128 devices in a mesh: tok: 64 (over x, y, z), head: 2 (over core).
Axes of the slice: x: 4, y: 4, z: 4, core: 2. Of those that a mesh axis runs over, the one named last changes fastest.
Arguments:
- queries: bfloat16 [2, 16384, 512], P('head', 'tok'), may hold values from -6 to 6
- key_rows: bfloat16 [2, 16384, 512], P('head', 'tok'), may hold values from -6 to 6
- value_rows: bfloat16 [2, 16384, 512], P('head', 'tok'), may hold values from -6 to 6
- step_rates: float32 [2, 16384], P('head', 'tok'), may hold values from 0.1 to 1
- w_gate: bfloat16 [2, 512, 512], P('head'), may hold values from -0.25 to 0.25
- w_up: bfloat16 [2, 512, 512], P('head'), may hold values from -0.25 to 0.25
- w_down: bfloat16 [2, 512, 512], P('head'), may hold values from -0.25 to 0.25
- out_gain: float32 [2, 512], P('head'), may hold values from 0.1 to 1.9
- cotangent: bfloat16 [2, 16384, 512], P('head', 'tok'), may hold values from -6 to 6
Outputs:
- grad_queries: bfloat16 [2, 16384, 512], P('head', 'tok')
- grad_keys: bfloat16 [2, 16384, 512], P('head', 'tok')
- grad_values: bfloat16 [2, 16384, 512], P('head', 'tok')
- grad_gate: float32 [2, 512, 512], P('head', 'tok')
- grad_up: float32 [2, 512, 512], P('head', 'tok')
- grad_down: float32 [2, 512, 512], P('head', 'tok')
The draws below stay inside these ranges and needn't reach their ends.
All inputs are finite; a program needn't handle non-finite values.
Results may differ from the reference program's by a relative error of at most 0.03.
Values sent between devices are 32-bit elements; how exact they have to be, the bound alone decides.
No kernel may reach another device: no remote copies, remote signals or barrier semaphores. Data moves between devices by JAX's collectives and lax.ppermute only.
A program may use at most 128 MiB of HBM per device.

```python
import math
import jax
import jax.numpy as jnp
from jax import lax

H = 2
DH = 512
NS_STEPS = 3
TOKENS = 16384


def level_of(own_key, extent, pieces, least, high):
    level, own = 1.0, jax.random.fold_in(own_key, 6)
    for position, shards_of in pieces:
        draws = jnp.exp(jax.random.uniform(jax.random.fold_in(own, position), (shards_of,), jnp.float32, least / len(pieces), high / len(pieces)))
        level = level * jnp.repeat(draws, extent[position] // shards_of).reshape([-1 if axis == position else 1 for axis in range(len(extent))])
    return level


def scatter_about(own_key, shape, deviation, bound, pieces=(), kind=jnp.bfloat16):
    drawn = jax.random.normal(own_key, shape, jnp.float32) * deviation
    if len(pieces) > 0:
        drawn = level_of(own_key, shape, pieces, -0.22, 0.18) * drawn
    return jnp.clip(drawn, min=-bound, max=bound).astype(kind)


def setup_inputs(seed: int = 0) -> dict:
    splits = jax.random.split(jax.random.key(seed), 10)
    return {
        "queries": scatter_about(splits[0], (H, TOKENS, DH), 1.0, 6.0, ((0, 2), (1, 64))),
        "key_rows": scatter_about(splits[1], (H, TOKENS, DH), 1.0, 6.0, ((0, 2), (1, 64))),
        "value_rows": scatter_about(splits[2], (H, TOKENS, DH), 1.0, 6.0, ((0, 2), (1, 64))),
        "step_rates": jnp.clip(jnp.exp(math.log(1.0) - 2.3025851 * jax.random.uniform(splits[3], (H, TOKENS), jnp.float32) ** level_of(splits[3], (H, TOKENS), ((0, 2), (1, 64)), -0.2, 0.2)), 0.1, 1.0),
        "w_gate": scatter_about(splits[4], (H, DH, DH), DH ** -0.5, 0.25, ((0, 2),)),
        "w_up": scatter_about(splits[5], (H, DH, DH), DH ** -0.5, 0.25, ((0, 2),)),
        "w_down": scatter_about(splits[6], (H, DH, DH), DH ** -0.5, 0.25, ((0, 2),)),
        "out_gain": jnp.clip(1.0 + 0.18 * jax.random.normal(splits[7], (H, DH), jnp.float32), 0.1, 1.9),
        "cotangent": scatter_about(splits[8], (H, TOKENS, DH), 1.0, 6.0, ((0, 2), (1, 64))),
    }


coef_first = 3.4445
coef_second = -4.775
coef_third = 2.0315
inner_step = 0.5

def contract_rows(first_op, second_op):
    return lax.dot_general(first_op, second_op, (((0,), (0,)), ((), ())), preferred_element_type=jnp.float32)

def contract_cols(first_op, second_op):
    return lax.dot_general(first_op, second_op, (((1,), (1,)), ((), ())), preferred_element_type=jnp.float32)

def silu_parts(pre_gate):
    sigma_gate = jax.nn.sigmoid(pre_gate)
    act_gate = pre_gate * sigma_gate
    slope_gate = sigma_gate * (1.0 + pre_gate * (1.0 - sigma_gate))
    return (act_gate, slope_gate, sigma_gate)

def orthogonalize(matrix):
    current = matrix / jnp.sqrt(jnp.sum(matrix * matrix) + 1e-06)
    for iteration in range(NS_STEPS):
        narrow = current.astype(jnp.bfloat16)
        gram_matrix = contract_cols(narrow, narrow)
        gram_low = gram_matrix.astype(jnp.bfloat16)
        poly_term = (coef_second * gram_matrix + coef_third * jnp.dot(gram_low, gram_low, preferred_element_type=jnp.float32)).astype(jnp.bfloat16)
        current = coef_first * current + jnp.dot(poly_term, narrow, preferred_element_type=jnp.float32)
    return current

def orthogonalize_all(grad_triple):
    mapped = jax.vmap(orthogonalize)
    return (mapped(grad_triple[0]), mapped(grad_triple[1]), mapped(grad_triple[2]))

def key_forward(w_gate, w_up, w_down, key_rows, value_rows, step_rates):
    key_gate = jnp.dot(key_rows, w_gate, preferred_element_type=jnp.float32)
    key_up = jnp.dot(key_rows, w_up, preferred_element_type=jnp.float32)
    act_gate, slope_gate, sigma_gate = silu_parts(key_gate)
    key_mixed = (act_gate * key_up).astype(jnp.bfloat16)
    target = (-step_rates[:, None] * value_rows).astype(jnp.bfloat16)
    key_mid = contract_cols(target, w_down)
    key_dgate = (key_mid * key_up * slope_gate).astype(jnp.bfloat16)
    key_dup = (key_mid * act_gate).astype(jnp.bfloat16)
    inner_grads = (contract_rows(key_rows, key_dgate), contract_rows(key_rows, key_dup), contract_rows(key_mixed, target))
    stored = (key_gate, key_up, act_gate, slope_gate, sigma_gate, key_mixed, target, key_mid, key_dgate, key_dup)
    return (inner_grads, stored)

def key_backward(w_gate, w_up, w_down, key_rows, step_rates, stored, back_a, back_b, back_c):
    key_gate, key_up, act_gate, slope_gate, sigma_gate, key_mixed, target, key_mid, key_dgate, key_dup = stored
    cot_a = back_a.astype(jnp.bfloat16)
    cot_b = back_b.astype(jnp.bfloat16)
    cot_c = back_c.astype(jnp.bfloat16)
    back_gate = jnp.dot(key_rows, cot_a, preferred_element_type=jnp.float32)
    back_up = jnp.dot(key_rows, cot_b, preferred_element_type=jnp.float32)
    back_mixed = contract_cols(target, cot_c)
    back_target = jnp.dot(key_mixed, cot_c, preferred_element_type=jnp.float32)
    curve_gate = sigma_gate * (1.0 - sigma_gate) * (2.0 + key_gate * (1.0 - 2.0 * sigma_gate))
    back_mid = (back_gate * key_up * slope_gate + back_up * act_gate).astype(jnp.bfloat16)
    gate_back = (back_gate * key_mid * key_up * curve_gate + back_up * key_mid * slope_gate + back_mixed * key_up * slope_gate).astype(jnp.bfloat16)
    up_back = (back_gate * key_mid * slope_gate + back_mixed * act_gate).astype(jnp.bfloat16)
    key_grad = contract_cols(key_dgate, cot_a) + contract_cols(key_dup, cot_b) + contract_cols(gate_back, w_gate) + contract_cols(up_back, w_up)
    value_sum = back_target + jnp.dot(back_mid, w_down, preferred_element_type=jnp.float32)
    value_grad = (-step_rates[:, None] * value_sum).astype(jnp.bfloat16)
    weight_terms = jnp.concatenate([contract_rows(key_rows, gate_back), contract_rows(key_rows, up_back), contract_rows(back_mid, target)], axis=1)
    return (key_grad.astype(jnp.bfloat16), value_grad, weight_terms)

def query_forward(new_gate, new_up, new_down, queries):
    query_gate = jnp.dot(queries, new_gate, preferred_element_type=jnp.float32)
    query_up = jnp.dot(queries, new_up, preferred_element_type=jnp.float32)
    act_gate, slope_gate, sigma_gate = silu_parts(query_gate)
    query_mixed = (act_gate * query_up).astype(jnp.bfloat16)
    output = jnp.dot(query_mixed, new_down, preferred_element_type=jnp.float32)
    return (output, (query_up, act_gate, slope_gate, query_mixed))

def query_backward(new_gate, new_up, new_down, queries, stored, grad_output):
    query_up, act_gate, slope_gate, query_mixed = stored
    query_mid = contract_cols(grad_output, new_down)
    query_dgate = (query_mid * query_up * slope_gate).astype(jnp.bfloat16)
    query_dup = (query_mid * act_gate).astype(jnp.bfloat16)
    query_grad = (contract_cols(query_dgate, new_gate) + contract_cols(query_dup, new_up)).astype(jnp.bfloat16)
    weight_terms = jnp.concatenate([contract_rows(queries, query_dgate), contract_rows(queries, query_dup), contract_rows(query_mixed, grad_output)], axis=1)
    return (query_grad, weight_terms)

def reference(queries, key_rows, value_rows, step_rates, w_gate, w_up, w_down, out_gain, cotangent):
    inner_grads, stored = jax.vmap(key_forward)(w_gate, w_up, w_down, key_rows, value_rows, step_rates)
    unitary, ns_back = jax.vjp(orthogonalize_all, inner_grads)
    new_gate = (w_gate - inner_step * unitary[0]).astype(jnp.bfloat16)
    new_up = (w_up - inner_step * unitary[1]).astype(jnp.bfloat16)
    new_down = (w_down - inner_step * unitary[2]).astype(jnp.bfloat16)
    output, query_stored = jax.vmap(query_forward)(new_gate, new_up, new_down, queries)
    full_width = H * DH
    squares = lax.optimization_barrier(jnp.sum(output * output, axis=(0, 2)))
    gain_wide = out_gain[:, None, :]
    aligned = lax.optimization_barrier(jnp.sum(cotangent * gain_wide * output, axis=(0, 2)))
    inverse_rms = lax.rsqrt(squares / full_width + 1e-05)
    grad_output = (gain_wide * cotangent * inverse_rms[None, :, None] - output * (aligned * inverse_rms * inverse_rms * inverse_rms / full_width)[None, :, None]).astype(jnp.bfloat16)
    query_grad, query_terms = jax.vmap(query_backward)(new_gate, new_up, new_down, queries, query_stored, grad_output)
    outer_back = (-inner_step * query_terms[:, :, :DH], -inner_step * query_terms[:, :, DH:2 * DH], -inner_step * query_terms[:, :, 2 * DH:])
    back_triple = ns_back(outer_back)[0]
    key_grad, value_grad, key_terms = jax.vmap(key_backward)(w_gate, w_up, w_down, key_rows, step_rates, stored, back_triple[0], back_triple[1], back_triple[2])
    weight_total = query_terms + key_terms
    return (query_grad, key_grad, value_grad, weight_total[:, :, :DH], weight_total[:, :, DH:2 * DH], weight_total[:, :, 2 * DH:])
```

```python
import functools

import jax
import jax.numpy as jnp
from jax import lax
from jax.experimental import pallas as pl
from jax.experimental.pallas import tpu as pltpu
from jax.sharding import Mesh
from jax.sharding import PartitionSpec as P

TOK = ("tok_0", "tok_1", "tok_2")
ALL = TOK + ("head",)
NS_STEPS = 3
DH = 512
WIDE = 3 * DH
BF = jnp.bfloat16
F32 = jnp.float32
coef_first = 3.4445
coef_second = -4.775
coef_third = 2.0315
inner_step = 0.5
VMEM_BYTES = 48 * 1024 * 1024


def flat_at(x, y, z, c):
    return ((x * 4 + y) * 4 + z) * 2 + c


def links(move):
    out = []
    for x in range(4):
        for y in range(4):
            for z in range(4):
                for c in range(2):
                    out.append((flat_at(x, y, z, c), flat_at(*move(x, y, z, c), c)))
    return out


def partner_links(level, step):
    if level == 3:
        flips = {1: lambda i: 3 - i, 2: lambda i: i ^ 1, 3: lambda i: i ^ 2}[step]
        return links(lambda x, y, z, c: (flips(x), flips(y), flips(z)))
    axis = 3 - step

    def move(x, y, z, c):
        at = [x, y, z]
        at[axis] = at[axis] ^ 1 if (level == 1) != (c == 1) else 3 - at[axis]
        return at

    return links(move)


PARTNERS = {(level, step): partner_links(level, step) for level in (1, 2, 3) for step in (1, 2, 3)}


def sent(value, level, step):
    return lax.ppermute(value, ALL, PARTNERS[level, step])


def low_bit(i):
    return ((i + 1) // 2) % 2


def high_bit(i):
    return i // 2


def colour(bit, x, y, z):
    code = bit(x) * 4 + bit(y) * 2 + bit(z)
    if isinstance(code, int):
        return (7 - code, 1) if code >= 4 else (code, 0)
    far = code // 4
    return jnp.where(far == 1, 7 - code, code), far


def own_colours():
    x, y, z = (lax.axis_index(a) for a in TOK)
    core = lax.axis_index("head")
    low, low_far = colour(low_bit, x, y, z)
    high, high_far = colour(high_bit, x, y, z)
    first = jnp.where(core == 0, low, high)
    second = jnp.where(core == 0, high, low)
    token = (x * 4 + y) * 4 + z
    return jnp.stack([first, second, low_far * 2 + high_far, token, core]).astype(jnp.int32)


def rows_order():
    orders = []
    for core in range(2):
        order = []
        for x in range(4):
            for y in range(4):
                for z in range(4):
                    low, low_far = colour(low_bit, x, y, z)
                    high, high_far = colour(high_bit, x, y, z)
                    first, second = (low, high) if core == 0 else (high, low)
                    order.append(first * 16 + second * 4 + low_far * 2 + high_far)
        orders.append(order)
    return orders


ORDERS = rows_order()


def call(body, outs, *args, scratch=(), scalars=None, flops=0):
    specs = [pl.BlockSpec(memory_space=pltpu.VMEM)] * len(args)
    if scalars is not None:
        specs = [pl.BlockSpec(memory_space=pltpu.SMEM)] + specs
        args = (scalars, *args)
    moved = sum(a.size * a.dtype.itemsize for a in args) + sum(
        o.size * o.dtype.itemsize for o in outs
    )
    return pl.pallas_call(
        body,
        out_shape=list(outs),
        in_specs=specs,
        out_specs=[pl.BlockSpec(memory_space=pltpu.VMEM)] * len(outs),
        scratch_shapes=list(scratch),
        compiler_params=pltpu.CompilerParams(vmem_limit_bytes=VMEM_BYTES),
        cost_estimate=pl.CostEstimate(flops=flops, bytes_accessed=moved, transcendentals=0),
    )(*args)


def shape(*dims, dtype=F32):
    return jax.ShapeDtypeStruct(dims, dtype)


def nn(a, b):
    return jnp.dot(a, b, preferred_element_type=F32)


def nt(a, b):
    return lax.dot_general(a, b, (((1,), (1,)), ((), ())), preferred_element_type=F32)


def tn(a, b):
    return lax.dot_general(a, b, (((0,), (0,)), ((), ())), preferred_element_type=F32)


def part(ref, index, rows):
    return ref[pl.ds(pl.multiple_of(index * rows, rows), rows), :]


def hand_out(own, whole, outs, rows):
    for step in range(4):
        outs[step][...] = part(whole, own ^ step, rows)


def fold_body(slot, rows, own, a, b, c, d, *outs):
    for step in range(4):
        at = own[slot] ^ step
        outs[step][...] = (part(a, at, rows) + part(b, at, rows)) + (
            part(c, at, rows) + part(d, at, rows)
        )


def total_body(a, b, c, d, out):
    out[...] = (a[...] + b[...]) + (c[...] + d[...])


def join_body(own, a, b, c, d, out):
    rows = a.shape[0]
    for step, piece in enumerate((a, b, c, d)):
        out[pl.ds(pl.multiple_of((own[1] ^ step) * rows, rows), rows), :] = piece[...]


def received(blocks, level):
    return [blocks[0]] + [sent(blocks[step], level, step) for step in (1, 2, 3)]


def sum_of_32(blocks, own):
    blocks = received(blocks, 1)
    blocks = call(
        functools.partial(fold_body, 1, 32), [shape(32, WIDE)] * 4, *blocks, scalars=own
    )
    return received(blocks, 2)


def sum_everywhere(blocks, own):
    blocks = sum_of_32(blocks, own)
    (piece,) = call(total_body, [shape(32, WIDE)], *blocks)
    (piece,) = call(total_body, [shape(32, WIDE)], *received([piece] * 4, 3))
    (piece,) = call(join_body, [shape(128, WIDE)], *received([piece] * 4, 2), scalars=own)
    return received([piece] * 4, 1)


def silu_parts(pre_gate):
    sigma_gate = jax.nn.sigmoid(pre_gate)
    act_gate = pre_gate * sigma_gate
    slope_gate = sigma_gate * (1.0 + pre_gate * (1.0 - sigma_gate))
    return (act_gate, slope_gate, sigma_gate)


def as_column(row):
    return jnp.transpose(jnp.broadcast_to(row, (128, row.shape[1])))[:, :1]


def key_body(own, w_gate, w_up, w_down, keys, values, rates, *refs):
    outs, stored, (whole,) = refs[:4], refs[4:11], refs[11:]
    gate, up, mid, mixed, target, dgate, dup = stored
    k = keys[...]
    t = (-as_column(rates[...]) * values[...].astype(F32)).astype(BF)
    target[...] = t
    g = nn(k, w_gate[...])
    u = nn(k, w_up[...])
    m = nt(t, w_down[...])
    gate[...] = g
    up[...] = u
    mid[...] = m
    act, slope, _ = silu_parts(g)
    mix = (act * u).astype(BF)
    dg = (m * u * slope).astype(BF)
    du = (m * act).astype(BF)
    mixed[...] = mix
    dgate[...] = dg
    dup[...] = du
    whole[:, :DH] = tn(k, dg)
    whole[:, DH : 2 * DH] = tn(k, du)
    whole[:, 2 * DH :] = tn(mix, t)
    hand_out(own[0], whole, outs, DH // 4)


def query_forward_body(new, queries, cotangent, gain, stats, output, act_out, slope_out, mixed):
    q = queries[...]
    g = nn(q, new[0])
    u = nn(q, new[1])
    act, slope, _ = silu_parts(g)
    mix = (act * u).astype(BF)
    out = nn(mix, new[2])
    squares = jnp.sum(out * out, axis=1, keepdims=True)
    aligned = jnp.sum(cotangent[...].astype(F32) * gain[...] * out, axis=1, keepdims=True)
    lane = lax.broadcasted_iota(jnp.int32, stats.shape, 1)
    stats[...] = jnp.where(lane == 0, squares, aligned)
    output[...] = out
    act_out[...] = act
    slope_out[...] = u * slope
    mixed[...] = mix


def query_backward_body(
    own, new, queries, cotangent, gain, stats, other, output, act, slope, mixed, *refs
):
    query_grad, outs, (whole,) = refs[0], refs[1:5], refs[5:]
    both = stats[...] + other[...]
    inverse_rms = lax.rsqrt(both[:, :1] / (2 * DH) + 1e-05)
    aligned = both[:, 1:2]
    grad_output = (
        gain[...] * cotangent[...].astype(F32) * inverse_rms
        - output[...] * (aligned * inverse_rms * inverse_rms * inverse_rms / (2 * DH))
    ).astype(BF)
    mid = nt(grad_output, new[2])
    dgate = (mid * slope[...]).astype(BF)
    dup = (mid * act[...]).astype(BF)
    query_grad[...] = (nt(dgate, new[0]) + nt(dup, new[1])).astype(BF)
    q = queries[...]
    whole[:, :DH] = tn(q, dgate)
    whole[:, DH : 2 * DH] = tn(q, dup)
    whole[:, 2 * DH :] = tn(mixed[...], grad_output)
    hand_out(own[0], whole, outs, DH // 4)


def key_backward_body(
    own, cots, w_gate, w_up, w_down, keys, rates, gate, up, mid, mixed, target, dgate, dup, *refs
):
    key_grad, value_grad, outs, (whole,) = refs[0], refs[1], refs[2:6], refs[6:]
    k = keys[...]
    t = target[...]
    cot_a, cot_b, cot_c = cots[0], cots[1], cots[2]
    back_gate = nn(k, cot_a)
    back_up = nn(k, cot_b)
    back_mixed = nt(t, cot_c)
    g = gate[...]
    u = up[...]
    m = mid[...]
    act, slope, sigma = silu_parts(g)
    curve = sigma * (1.0 - sigma) * (2.0 + g * (1.0 - 2.0 * sigma))
    back_mid = (back_gate * u * slope + back_up * act).astype(BF)
    gate_back = (
        back_gate * m * u * curve + back_up * m * slope + back_mixed * u * slope
    ).astype(BF)
    up_back = (back_gate * m * slope + back_mixed * act).astype(BF)
    whole[:, :DH] = tn(k, gate_back)
    whole[:, DH : 2 * DH] = tn(k, up_back)
    whole[:, 2 * DH :] = tn(back_mid, t)
    key_grad[...] = (
        nt(dgate[...], cot_a)
        + nt(dup[...], cot_b)
        + nt(gate_back, w_gate[...])
        + nt(up_back, w_up[...])
    ).astype(BF)
    value_sum = nn(mixed[...], cot_c) + nn(back_mid, w_down[...])
    value_grad[...] = (-as_column(rates[...]) * value_sum).astype(BF)
    first = own[0]
    for step in range(4):
        for t_in in range(16):
            block = (first ^ step) * 16 + t_in
            source = own[8 + block]
            outs[step][8 * t_in : 8 * t_in + 8, :] = part(whole, source, 8)


def share_body(share, a, b, c, d, out_a, out_b, out_c):
    value = share[...] + ((a[...] + b[...]) + (c[...] + d[...]))
    out_a[0] = value[:, :DH]
    out_b[0] = value[:, DH : 2 * DH]
    out_c[0] = value[:, 2 * DH :]


def gather_in(own, blocks, whole):
    rows = DH // 4
    for step, block in enumerate(blocks):
        whole[pl.ds(pl.multiple_of((own[0] ^ step) * rows, rows), rows), :] = block[...]


def ortho_body(own, a, b, c, d, w_gate, w_up, w_down, new, kept, norm, whole):
    gather_in(own, (a, b, c, d), whole)
    matrix = whole[...]
    root = jnp.sqrt(jnp.sum(matrix * matrix, keepdims=True) + 1e-06)
    current = matrix * (1.0 / root)
    for step in range(NS_STEPS):
        narrow = current.astype(BF)
        gram = nt(narrow, narrow)
        gram_low = gram.astype(BF)
        poly = (coef_second * gram + coef_third * nn(gram_low, gram_low)).astype(BF)
        kept[3 * step] = narrow
        kept[3 * step + 1] = gram_low
        kept[3 * step + 2] = poly
        current = coef_first * current + nn(poly, narrow)
    norm[...] = jnp.broadcast_to(root, norm.shape)
    for index, weight in enumerate((w_gate, w_up, w_down)):

        @pl.when(pl.program_id(0) == index)
        def _():
            new[...] = (weight[...].astype(F32) - inner_step * current).astype(BF)


def ortho_back_body(own, a, b, c, d, kept, norm, cots, share, whole):
    gather_in(own, (a, b, c, d), whole)
    share[...] = part(whole, own[3], 8)
    grad = whole[...] * (-inner_step)
    for step in reversed(range(NS_STEPS)):
        narrow, gram_low, poly = kept[3 * step], kept[3 * step + 1], kept[3 * step + 2]
        grad_low = grad.astype(BF)
        half = nt(grad_low, narrow)
        sym = half + jnp.transpose(half)
        cross = nn(sym.astype(BF), gram_low)
        full = coef_second * sym + coef_third * (cross + jnp.transpose(cross))
        grad = coef_first * grad + nn(poly, grad_low) + nn(full.astype(BF), narrow)
    unit = kept[0].astype(F32)
    along = jnp.sum(grad * unit, keepdims=True)
    cots[...] = ((grad - unit * along) * (1.0 / norm[:1, :1])).astype(BF)


def one_of_three(*dims):
    return pl.BlockSpec((None, *dims), lambda i: (i,) + (0,) * len(dims))


SMEM = pl.BlockSpec(memory_space=pltpu.SMEM)
QUARTERS = [pl.BlockSpec((DH // 4, DH), lambda i: (0, i))] * 4
WHOLE = pl.BlockSpec((DH, DH), lambda i: (0, 0))
PARAMS = pltpu.CompilerParams(vmem_limit_bytes=VMEM_BYTES)


def ortho(blocks, own, w_gate, w_up, w_down):
    return pl.pallas_call(
        ortho_body,
        grid=(3,),
        in_specs=[SMEM, *QUARTERS, WHOLE, WHOLE, WHOLE],
        out_specs=[one_of_three(DH, DH), one_of_three(9, DH, DH), one_of_three(8, 128)],
        out_shape=[shape(3, DH, DH, dtype=BF), shape(3, 9, DH, DH, dtype=BF), shape(3, 8, 128)],
        scratch_shapes=[pltpu.VMEM((DH, DH), F32)],
        compiler_params=PARAMS,
    )(own, *blocks, w_gate, w_up, w_down)


def ortho_back(blocks, own, kept, norm):
    return pl.pallas_call(
        ortho_back_body,
        grid=(3,),
        in_specs=[SMEM, *QUARTERS, one_of_three(9, DH, DH), one_of_three(8, 128)],
        out_specs=[one_of_three(DH, DH), pl.BlockSpec((8, DH), lambda i: (0, i))],
        out_shape=[shape(3, DH, DH, dtype=BF), shape(8, WIDE)],
        scratch_shapes=[pltpu.VMEM((DH, DH), F32)],
        compiler_params=PARAMS,
    )(own, *blocks, kept, norm)


def local(queries, key_rows, value_rows, step_rates, w_gate, w_up, w_down, out_gain, cotangent):
    tokens = queries.shape[1]
    queries, key_rows, value_rows, cotangent = (
        a[0] for a in (queries, key_rows, value_rows, cotangent)
    )
    w_gate, w_up, w_down = w_gate[0], w_up[0], w_down[0]
    own = own_colours()
    inverse = jnp.asarray(
        [[order.index(block) for block in range(64)] for order in ORDERS], jnp.int32
    )
    own = jnp.concatenate([own, jnp.zeros(3, jnp.int32), inverse[own[4]]])

    whole = pltpu.VMEM((DH, WIDE), F32)
    quarters = [shape(DH // 4, WIDE)] * 4
    wide = shape(tokens, DH)
    low = shape(tokens, DH, dtype=BF)
    *blocks, gate, up, mid, mixed, target, dgate, dup = call(
        key_body,
        [*quarters, wide, wide, wide, low, low, low, low],
        w_gate,
        w_up,
        w_down,
        key_rows,
        value_rows,
        step_rates,
        scratch=[whole],
        scalars=own,
    )
    new, kept, norm = ortho(sum_everywhere(blocks, own), own, w_gate, w_up, w_down)
    stats, *query_stored = call(
        query_forward_body,
        [shape(tokens, 128), wide, wide, wide, low],
        new,
        queries,
        cotangent,
        out_gain,
    )
    swap = links(lambda x, y, z, c: (x, y, z))
    swap = [(source, target_at ^ 1) for source, target_at in swap]
    other = lax.ppermute(stats, ALL, swap)
    query_grad, *blocks = call(
        query_backward_body,
        [low, *quarters],
        new,
        queries,
        cotangent,
        out_gain,
        stats,
        other,
        *query_stored,
        scratch=[whole],
        scalars=own,
    )
    cots, share = ortho_back(sum_everywhere(blocks, own), own, kept, norm)
    key_grad, value_grad, *blocks = call(
        key_backward_body,
        [low, low, *quarters],
        cots,
        w_gate,
        w_up,
        w_down,
        key_rows,
        step_rates,
        gate,
        up,
        mid,
        mixed,
        target,
        dgate,
        dup,
        scratch=[whole],
        scalars=own,
    )
    blocks = sum_of_32(blocks, own)
    blocks = call(
        functools.partial(fold_body, 2, 8), [shape(8, WIDE)] * 4, *blocks, scalars=own
    )
    grads = call(share_body, [shape(1, 8, DH)] * 3, share, *received(blocks, 3))
    return (query_grad[None], key_grad[None], value_grad[None], *grads)


def solution(mesh):
    split = Mesh(
        mesh.devices.reshape(4, 4, 4, mesh.shape["head"]), ("tok_0", "tok_1", "tok_2", "head")
    )
    rows = P("head", TOK, None)
    weight = P("head", None, None)
    in_specs = (
        rows,
        rows,
        rows,
        P("head", TOK),
        weight,
        weight,
        weight,
        P("head", None),
        rows,
    )
    return jax.shard_map(
        local, mesh=split, in_specs=in_specs, out_specs=(rows,) * 6, check_vma=False
    )
```

```python
import jax
import jax.numpy as jnp
from jax import lax
from jax.experimental import pallas as pl
from jax.experimental.pallas import tpu as pltpu
from jax.sharding import Mesh
from jax.sharding import PartitionSpec as P

TOK = ("tok_0", "tok_1", "tok_2")
ALL = TOK + ("head",)
NS_STEPS = 3
DH = 512
WIDE = 3 * DH
BF = jnp.bfloat16
F32 = jnp.float32
coef_first = 3.4445
coef_second = -4.775
coef_third = 2.0315
inner_step = 0.5
VMEM_BYTES = 24 * 1024 * 1024


def flat_at(x, y, z, c):
    return ((x * 4 + y) * 4 + z) * 2 + c


def links(move):
    out = []
    for x in range(4):
        for y in range(4):
            for z in range(4):
                for c in range(2):
                    out.append((flat_at(x, y, z, c), flat_at(*move(x, y, z, c))))
    return out


def pair(i, near):
    return i ^ 1 if near else 3 - i


def partner_links(level, step):
    axis = 3 - step

    def move(x, y, z, c):
        at = [x, y, z]
        at[axis] = pair(at[axis], (level == 1) != (c == 1))
        return (*at, c)

    return links(move)


def antipode_links(level):
    def move(x, y, z, c):
        near = (level == 1) != (c == 1)
        return (pair(x, near), pair(y, near), pair(z, near), c)

    return links(move)


PARTNERS = {(level, step): partner_links(level, step) for level in (1, 2) for step in (1, 2, 3)}
ANTIPODES = {level: antipode_links(level) for level in (1, 2)}
OTHER_CORE = links(lambda x, y, z, c: (x, y, z, 1 - c))


def colour(bit, x, y, z):
    code = bit(x) * 4 + bit(y) * 2 + bit(z)
    return jnp.where(code >= 4, 7 - code, code)


def own_colours():
    x, y, z = (lax.axis_index(a) for a in TOK)
    core = lax.axis_index("head")
    low = colour(lambda i: ((i + 1) // 2) % 2, x, y, z)
    high = colour(lambda i: i // 2, x, y, z)
    first = jnp.where(core == 0, low, high)
    second = jnp.where(core == 0, high, low)
    token = (x * 4 + y) * 4 + z
    return jnp.stack([first, second, token]).astype(jnp.int32)


SMEM = pl.BlockSpec(memory_space=pltpu.SMEM)
VMEM = pl.BlockSpec(memory_space=pltpu.VMEM)
HBM = pl.BlockSpec(memory_space=pl.ANY)


def call(body, outs, *args, scratch=(), scalars=None, flops=0, specs=None, limit=VMEM_BYTES):
    specs = specs or [VMEM] * len(args)
    if scalars is not None:
        specs = [SMEM] + specs
        args = (scalars, *args)
    moved = sum(a.size * a.dtype.itemsize for a in args) + sum(
        o.size * o.dtype.itemsize for o in outs
    )
    return pl.pallas_call(
        body,
        out_shape=list(outs),
        in_specs=specs,
        out_specs=[VMEM] * len(outs),
        scratch_shapes=list(scratch),
        compiler_params=pltpu.CompilerParams(vmem_limit_bytes=limit),
        cost_estimate=pl.CostEstimate(flops=flops, bytes_accessed=moved, transcendentals=0),
    )(*args)


def shape(*dims, dtype=F32):
    return jax.ShapeDtypeStruct(dims, dtype)


def nn(a, b):
    return jnp.dot(a, b, preferred_element_type=F32)


def nt(a, b):
    return lax.dot_general(a, b, (((1,), (1,)), ((), ())), preferred_element_type=F32)


def tn(a, b):
    return lax.dot_general(a, b, (((0,), (0,)), ((), ())), preferred_element_type=F32)


def rows_at(index, rows):
    return pl.ds(pl.multiple_of(index * rows, rows), rows)


def hand_out(own, whole, outs, rows):
    for step in range(4):
        outs[step][...] = whole[rows_at(own ^ step, rows), :]


def fold_body(own, a, b, c, d, *outs):
    rows = outs[0].shape[0]
    for step in range(4):
        at = rows_at(own[1] ^ step, rows)
        outs[step][...] = (a[at, :] + b[at, :]) + (c[at, :] + d[at, :])


def total_body(*refs):
    *parts, out = refs
    values = [part[...] for part in parts]
    while len(values) > 1:
        values = [values[i] + values[i + 1] for i in range(0, len(values), 2)]
    out[...] = values[0]


def join_body(own, a, b, c, d, out):
    rows = a.shape[0]
    for step, piece in enumerate((a, b, c, d)):
        out[rows_at(own[1] ^ step, rows), :] = piece[...]


def received(blocks, level):
    return [blocks[0]] + [
        lax.ppermute(blocks[step], ALL, PARTNERS[level, step]) for step in (1, 2, 3)
    ]


def sum_everywhere(blocks, own):
    piece_shape = [shape(32, WIDE)]
    blocks = received(blocks, 1)
    blocks = call(fold_body, piece_shape * 4, *blocks, scalars=own)
    (piece,) = call(total_body, piece_shape, *received(blocks, 2))
    for level in (1, 2):
        arrived = lax.ppermute(piece, ALL, ANTIPODES[level])
        (piece,) = call(total_body, piece_shape, piece, arrived)
    (piece,) = call(join_body, [shape(128, WIDE)], *received([piece] * 4, 2), scalars=own)
    return received([piece] * 4, 1)


def silu_parts(pre_gate):
    sigma_gate = jax.nn.sigmoid(pre_gate)
    act_gate = pre_gate * sigma_gate
    slope_gate = sigma_gate * (1.0 + pre_gate * (1.0 - sigma_gate))
    return (act_gate, slope_gate, sigma_gate)


def as_column(row):
    return jnp.transpose(jnp.broadcast_to(row, (128, row.shape[1])))[:, :1]


def key_body(own, rates, *refs):
    sources, outs, stored = refs[:5], refs[5:9], refs[9:16]
    whole, copies, sems = refs[16], refs[17:22], refs[22]
    gate, up, mid, mixed, target, dgate, dup = stored
    moves = [
        pltpu.make_async_copy(source, copy, sems.at[i])
        for i, (source, copy) in enumerate(zip(sources, copies))
    ]
    for move in moves:
        move.start()
    keys, w_gate, w_up, values, w_down = copies
    moves[0].wait()
    moves[1].wait()
    k = keys[...]
    g = nn(k, w_gate[...])
    gate[...] = g
    moves[2].wait()
    u = nn(k, w_up[...])
    up[...] = u
    act, slope, _ = silu_parts(g)
    mix = (act * u).astype(BF)
    mixed[...] = mix
    moves[3].wait()
    t = (-as_column(rates[...]) * values[...].astype(F32)).astype(BF)
    target[...] = t
    whole[:, 2 * DH :] = tn(mix, t)
    moves[4].wait()
    m = nt(t, w_down[...])
    mid[...] = m
    dg = (m * u * slope).astype(BF)
    du = (m * act).astype(BF)
    dgate[...] = dg
    dup[...] = du
    whole[:, :DH] = tn(k, dg)
    whole[:, DH : 2 * DH] = tn(k, du)
    hand_out(own[0], whole, outs, DH // 4)


def query_forward(new, queries, cotangent, gain, stats, output, act_out, slope_out, mixed):
    q = queries[...]
    g = nn(q, new[0])
    u = nn(q, new[1])
    act, slope, _ = silu_parts(g)
    mix = (act * u).astype(BF)
    out = nn(mix, new[2])
    squares = jnp.sum(out * out, axis=1, keepdims=True)
    aligned = jnp.sum(cotangent[...].astype(F32) * gain[...] * out, axis=1, keepdims=True)
    lane = lax.broadcasted_iota(jnp.int32, stats.shape, 1)
    stats[...] = jnp.where(lane == 0, squares, aligned)
    output[...] = out
    act_out[...] = act
    slope_out[...] = u * slope
    mixed[...] = mix


def query_terms_body(
    own, w_down, queries, cotangent, gain, stats, other, output, act, slope, mixed, *refs
):
    outs, dgate, dup, whole = refs[:4], refs[4], refs[5], refs[6]
    both = stats[...] + other[...]
    inverse_rms = lax.rsqrt(both[:, :1] / (2 * DH) + 1e-05)
    aligned = both[:, 1:2]
    grad_output = (
        gain[...] * cotangent[...].astype(F32) * inverse_rms
        - output[...] * (aligned * inverse_rms * inverse_rms * inverse_rms / (2 * DH))
    ).astype(BF)
    mid = nt(grad_output, w_down[2])
    dg = (mid * slope[...]).astype(BF)
    du = (mid * act[...]).astype(BF)
    dgate[...] = dg
    dup[...] = du
    q = queries[...]
    whole[:, 2 * DH :] = tn(mixed[...], grad_output)
    whole[:, :DH] = tn(q, dg)
    whole[:, DH : 2 * DH] = tn(q, du)
    hand_out(own[0], whole, outs, DH // 4)


def query_grad_body(new, dgate, dup, query_grad):
    query_grad[...] = (nt(dgate[...], new[0]) + nt(dup[...], new[1])).astype(BF)


def key_terms(cots, keys, gate, up, mid, target, terms, back_mid, gate_back, up_back):
    k = keys[...]
    t = target[...]
    back_gate = nn(k, cots[0])
    back_up = nn(k, cots[1])
    back_mixed = nt(t, cots[2])
    g = gate[...]
    u = up[...]
    m = mid[...]
    act, slope, sigma = silu_parts(g)
    curve = sigma * (1.0 - sigma) * (2.0 + g * (1.0 - 2.0 * sigma))
    bm = (back_gate * u * slope + back_up * act).astype(BF)
    gb = (back_gate * m * u * curve + back_up * m * slope + back_mixed * u * slope).astype(BF)
    ub = (back_gate * m * slope + back_mixed * act).astype(BF)
    back_mid[...] = bm
    gate_back[...] = gb
    up_back[...] = ub
    terms[:, :DH] = tn(k, gb)
    terms[:, DH : 2 * DH] = tn(k, ub)
    terms[:, 2 * DH :] = tn(bm, t)


def key_grads_body(
    cots, w_gate, w_up, w_down, rates, mixed, dgate, dup, back_mid, gate_back, up_back, *outs
):
    key_grad, value_grad = outs
    key_grad[...] = (
        nt(dgate[...], cots[0])
        + nt(dup[...], cots[1])
        + nt(gate_back[...], w_gate[...])
        + nt(up_back[...], w_up[...])
    ).astype(BF)
    value_sum = nn(mixed[...], cots[2]) + nn(back_mid[...], w_down[...])
    value_grad[...] = (-as_column(rates[...]) * value_sum).astype(BF)


SHARE_STEPS = 4


def share_body(share, pieces, out_a, out_b, out_c, total):
    step = pl.program_id(0)

    @pl.when(step == 0)
    def _():
        total[...] = share[...]

    total[...] += jnp.sum(pieces[...], axis=0)

    @pl.when(step == SHARE_STEPS - 1)
    def _():
        out_a[0] = total[:, :DH]
        out_b[0] = total[:, DH : 2 * DH]
        out_c[0] = total[:, 2 * DH :]


def weight_shares(share, pieces):
    out = pl.BlockSpec((1, 8, DH), lambda i: (0, 0, 0))
    return pl.pallas_call(
        share_body,
        grid=(SHARE_STEPS,),
        in_specs=[
            pl.BlockSpec((8, WIDE), lambda i: (0, 0)),
            pl.BlockSpec((pieces.shape[0] // SHARE_STEPS, 8, WIDE), lambda i: (i, 0, 0)),
        ],
        out_specs=[out] * 3,
        out_shape=[shape(1, 8, DH)] * 3,
        scratch_shapes=[pltpu.VMEM((8, WIDE), F32)],
        compiler_params=pltpu.CompilerParams(vmem_limit_bytes=VMEM_BYTES),
    )(share, pieces)


EACH = range(3)


def columns(index):
    return slice(index * DH, (index + 1) * DH)


def ortho_body(own, a, b, c, d, w_gate, w_up, w_down, queries, cotangent, gain, *refs):
    new, kept, norm, query_refs, (current, gram) = refs[0], refs[1], refs[2], refs[3:8], refs[8:]
    for step, block in enumerate((a, b, c, d)):
        for i in EACH:
            current[i, rows_at(own[0] ^ step, DH // 4), :] = block[:, columns(i)]
    for i in EACH:
        matrix = current[i]
        root = jnp.sqrt(jnp.sum(matrix * matrix, keepdims=True) + 1e-06)
        norm[i] = jnp.broadcast_to(root, norm.shape[1:])
        unit = matrix * (1.0 / root)
        current[i] = unit
        kept[i, 0] = unit.astype(BF)
    for step in range(NS_STEPS):
        for i in EACH:
            narrow = kept[i, 3 * step]
            square = nt(narrow, narrow)
            gram[i] = square
            kept[i, 3 * step + 1] = square.astype(BF)
        for i in EACH:
            low = kept[i, 3 * step + 1]
            kept[i, 3 * step + 2] = (coef_second * gram[i] + coef_third * nn(low, low)).astype(BF)
        for i, weight in enumerate((w_gate, w_up, w_down)):
            later = coef_first * current[i] + nn(kept[i, 3 * step + 2], kept[i, 3 * step])
            if step < NS_STEPS - 1:
                current[i] = later
                kept[i, 3 * step + 3] = later.astype(BF)
            else:
                new[i] = (weight[...].astype(F32) - inner_step * later).astype(BF)
    query_forward(new, queries, cotangent, gain, *query_refs)


def ortho_back_body(own, a, b, c, d, kept, norm, keys, gate, up, mid, target, *refs):
    cots, share, terms, key_refs, (grad, grad_low, half, sym) = (
        refs[0],
        refs[1],
        refs[2],
        refs[3:6],
        refs[6:],
    )
    for step, block in enumerate((a, b, c, d)):
        for i in EACH:
            grad[i, rows_at(own[0] ^ step, DH // 4), :] = block[:, columns(i)]
    for i in EACH:
        share[:, columns(i)] = grad[i, rows_at(own[2], 8), :]
        start = grad[i] * (-inner_step)
        grad[i] = start
        grad_low[i] = start.astype(BF)
    for step in reversed(range(NS_STEPS)):
        for i in EACH:
            half[i] = nt(grad_low[i], kept[i, 3 * step])
        for i in EACH:
            both = half[i] + jnp.transpose(half[i])
            sym[i] = both.astype(BF)
        for i in EACH:
            half[i] = coef_third * nn(sym[i], kept[i, 3 * step + 1])
        for i in EACH:
            full = coef_second * sym[i].astype(F32) + (half[i] + jnp.transpose(half[i]))
            sym[i] = full.astype(BF)
        for i in EACH:
            later = (
                coef_first * grad[i]
                + nn(kept[i, 3 * step + 2], grad_low[i])
                + nn(sym[i], kept[i, 3 * step])
            )
            grad[i] = later
            if step > 0:
                grad_low[i] = later.astype(BF)
    for i in EACH:
        unit = kept[i, 0].astype(F32)
        along = jnp.sum(grad[i] * unit, keepdims=True)
        cots[i] = ((grad[i] - unit * along) * (1.0 / norm[i, :1, :1])).astype(BF)
    key_terms(cots, keys, gate, up, mid, target, terms, *key_refs)


def local(queries, key_rows, value_rows, step_rates, w_gate, w_up, w_down, out_gain, cotangent):
    tokens = queries.shape[1]
    queries, key_rows, value_rows, cotangent = (
        a[0] for a in (queries, key_rows, value_rows, cotangent)
    )
    w_gate, w_up, w_down = w_gate[0], w_up[0], w_down[0]
    own = own_colours()

    whole = pltpu.VMEM((DH, WIDE), F32)
    quarters = [shape(DH // 4, WIDE)] * 4
    wide = shape(tokens, DH)
    low = shape(tokens, DH, dtype=BF)
    three = shape(3, DH, DH, dtype=BF)
    three_f32 = pltpu.VMEM((3, DH, DH), F32)
    three_low = pltpu.VMEM((3, DH, DH), BF)
    token_low = pltpu.VMEM((tokens, DH), BF)
    square_low = pltpu.VMEM((DH, DH), BF)
    *blocks, gate, up, mid, mixed, target, dgate, dup = call(
        key_body,
        [*quarters, wide, wide, wide, low, low, low, low],
        step_rates,
        key_rows,
        w_gate,
        w_up,
        value_rows,
        w_down,
        scratch=[
            whole,
            token_low,
            square_low,
            square_low,
            token_low,
            square_low,
            pltpu.SemaphoreType.DMA((5,)),
        ],
        scalars=own,
        specs=[VMEM] + [HBM] * 5,
    )
    new, kept, norm, stats, *query_stored = call(
        ortho_body,
        [
            three,
            shape(3, 9, DH, DH, dtype=BF),
            shape(3, 8, 128),
            shape(tokens, 128),
            wide,
            wide,
            wide,
            low,
        ],
        *sum_everywhere(blocks, own),
        w_gate,
        w_up,
        w_down,
        queries,
        cotangent,
        out_gain,
        scalars=own,
        scratch=[three_f32, three_f32],
    )
    other = lax.ppermute(stats, ALL, OTHER_CORE)
    *blocks, query_dgate, query_dup = call(
        query_terms_body,
        [*quarters, low, low],
        new,
        queries,
        cotangent,
        out_gain,
        stats,
        other,
        *query_stored,
        scratch=[whole],
        scalars=own,
    )
    (query_grad,) = call(
        query_grad_body, [low], new, query_dgate, query_dup, flops=4 * tokens * DH * DH
    )
    cots, share, terms, back_mid, gate_back, up_back = call(
        ortho_back_body,
        [three, shape(8, WIDE), shape(DH, WIDE), low, low, low],
        *sum_everywhere(blocks, own),
        kept,
        norm,
        key_rows,
        gate,
        up,
        mid,
        target,
        scalars=own,
        scratch=[three_f32, three_low, three_f32, three_low],
    )
    devices = lax.axis_size(TOK)
    pieces = lax.all_to_all(
        terms.reshape(devices, DH // devices, WIDE), TOK, 0, 0, tiled=True
    )
    key_grad, value_grad = call(
        key_grads_body,
        [low, low],
        cots,
        w_gate,
        w_up,
        w_down,
        step_rates,
        mixed,
        dgate,
        dup,
        back_mid,
        gate_back,
        up_back,
        flops=12 * tokens * DH * DH,
    )
    grads = weight_shares(share, pieces)
    return (query_grad[None], key_grad[None], value_grad[None], *grads)


def solution(mesh):
    split = Mesh(
        mesh.devices.reshape(4, 4, 4, mesh.shape["head"]), ("tok_0", "tok_1", "tok_2", "head")
    )
    rows = P("head", TOK, None)
    weight = P("head", None, None)
    in_specs = (
        rows,
        rows,
        rows,
        P("head", TOK),
        weight,
        weight,
        weight,
        P("head", None),
        rows,
    )
    return jax.shard_map(
        local, mesh=split, in_specs=in_specs, out_specs=(rows,) * 6, check_vma=False
    )
```

```python
import jax
import jax.numpy as jnp
from jax import lax
from jax.experimental import pallas as pl
from jax.experimental.pallas import tpu as pltpu
from jax.sharding import Mesh
from jax.sharding import PartitionSpec as P

TOK = ("tok_0", "tok_1", "tok_2")
ALL = TOK + ("head",)
NS_STEPS = 3
DH = 512
WIDE = 3 * DH
BF = jnp.bfloat16
F32 = jnp.float32
coef_first = 3.4445
coef_second = -4.775
coef_third = 2.0315
inner_step = 0.5
VMEM_BYTES = 24 * 1024 * 1024


def flat_at(x, y, z, c):
    return ((x * 4 + y) * 4 + z) * 2 + c


def links(move):
    out = []
    for x in range(4):
        for y in range(4):
            for z in range(4):
                for c in range(2):
                    out.append((flat_at(x, y, z, c), flat_at(*move(x, y, z, c))))
    return out


def pair(i, near):
    return i ^ 1 if near else 3 - i


def partner_links(step):
    axis = 3 - step

    def move(x, y, z, c):
        at = [x, y, z]
        at[axis] = pair(at[axis], c == 0)
        return (*at, c)

    return links(move)


PARTNERS = {step: partner_links(step) for step in (1, 2, 3)}
OTHER_CORE = links(lambda x, y, z, c: (x, y, z, 1 - c))


def colour(x, y, z, c):
    code = 0
    for at in (x, y, z):
        code = 2 * code + (((at + 1) // 2) % 2 if c == 0 else at // 2)
    return min(code, 7 - code)


def places():
    return [(x, y, z) for x in range(4) for y in range(4) for z in range(4)]


def of_colour(wanted, c):
    return [at for at in places() if colour(*at, c) == wanted]


COLOUR_GROUPS = [[flat_at(*at, c) for at in of_colour(q, c)] for c in range(2) for q in range(4)]
COLOURS = [[colour(*at, c) for at in places()] for c in range(2)]
TOKENS_BY_COLOUR = [
    [places().index(at) for q in range(4) for at in of_colour(q, c)] for c in range(2)
]


def own_table():
    core = lax.axis_index("head")
    own = jnp.asarray(COLOURS, jnp.int32)[core, lax.axis_index(TOK)]
    return jnp.concatenate([own[None], jnp.asarray(TOKENS_BY_COLOUR, jnp.int32)[core]])


SMEM = pl.BlockSpec(memory_space=pltpu.SMEM)
VMEM = pl.BlockSpec(memory_space=pltpu.VMEM)
HBM = pl.BlockSpec(memory_space=pltpu.HBM)


def call(body, outs, *args, scratch=(), scalars=None, flops=0, specs=None, out_specs=None):
    specs = specs or [VMEM] * len(args)
    if scalars is not None:
        specs = [SMEM] + specs
        args = (scalars, *args)
    moved = sum(a.size * a.dtype.itemsize for a in args) + sum(
        o.size * o.dtype.itemsize for o in outs
    )
    return pl.pallas_call(
        body,
        out_shape=list(outs),
        in_specs=specs,
        out_specs=out_specs or [VMEM] * len(outs),
        scratch_shapes=list(scratch),
        compiler_params=pltpu.CompilerParams(vmem_limit_bytes=VMEM_BYTES),
        cost_estimate=pl.CostEstimate(flops=flops, bytes_accessed=moved, transcendentals=0),
    )(*args)


def shape(*dims, dtype=F32):
    return jax.ShapeDtypeStruct(dims, dtype)


def nn(a, b):
    return jnp.dot(a, b, preferred_element_type=F32)


def nt(a, b):
    return lax.dot_general(a, b, (((1,), (1,)), ((), ())), preferred_element_type=F32)


def tn(a, b):
    return lax.dot_general(a, b, (((0,), (0,)), ((), ())), preferred_element_type=F32)


def rows_at(index, rows):
    return pl.ds(pl.multiple_of(index * rows, rows), rows)


def send_part(whole, terms, sems, index):
    at = (slice(None), columns(index))
    copy = pltpu.make_async_copy(whole.at[at], terms.at[at], sems.at[index])
    copy.start()
    return copy


def columns(index):
    return slice(index * DH, (index + 1) * DH)


SUM_STEPS = 4


def sum_body(pieces, copies, total):
    step = pl.program_id(0)
    part = jnp.sum(pieces[...], axis=0)

    @pl.when(step == 0)
    def _():
        total[...] = part

    @pl.when(step > 0)
    def _():
        total[...] += part

    @pl.when(step == SUM_STEPS - 1)
    def _():
        copies[...] = jnp.broadcast_to(total[...], copies.shape)


def pieces_spec(pieces):
    return pl.BlockSpec((pieces.shape[0] // SUM_STEPS, 8, WIDE), lambda i: (i, 0, 0))


def to_owners(terms):
    devices = lax.axis_size(TOK)
    return lax.all_to_all(terms.reshape(devices, DH // devices, WIDE), TOK, 0, 0, tiled=True)


def sum_everywhere(terms):
    pieces = to_owners(terms)
    copies, share = pl.pallas_call(
        sum_body,
        grid=(SUM_STEPS,),
        in_specs=[pieces_spec(pieces)],
        out_specs=[
            pl.BlockSpec((16, 8, WIDE), lambda i: (0, 0, 0)),
            pl.BlockSpec((8, WIDE), lambda i: (0, 0)),
        ],
        out_shape=[shape(16, 8, WIDE), shape(8, WIDE)],
        compiler_params=pltpu.CompilerParams(vmem_limit_bytes=VMEM_BYTES),
    )(pieces)
    mine = lax.all_to_all(copies, ALL, 0, 0, axis_index_groups=COLOUR_GROUPS, tiled=True)
    mine = mine.reshape(DH // 4, WIDE)
    return [mine] + [lax.ppermute(mine, ALL, PARTNERS[step]) for step in (1, 2, 3)], share


def place_rows(own, blocks, matrices):
    for step, block in enumerate(blocks):
        first = 1 + 16 * (own[0] ^ step)
        for j in range(16):
            at = rows_at(own[first + j], 8)
            for i in EACH:
                matrices[i, at, :] = block[8 * j : 8 * j + 8, columns(i)]


EACH = range(3)


def silu_parts(pre_gate):
    sigma_gate = jax.nn.sigmoid(pre_gate)
    act_gate = pre_gate * sigma_gate
    slope_gate = sigma_gate * (1.0 + pre_gate * (1.0 - sigma_gate))
    return (act_gate, slope_gate, sigma_gate)


def as_column(row):
    return jnp.transpose(jnp.broadcast_to(row, (128, row.shape[1])))[:, :1]


def key_body(rates, *refs):
    sources, terms, stored = refs[:5], refs[5], refs[6:13]
    whole, copies, sems, out_sems = refs[13], refs[14:19], refs[19], refs[20]
    gate, up, mid, mixed, target, dgate, dup = stored
    moves = [
        pltpu.make_async_copy(source, copy, sems.at[i])
        for i, (source, copy) in enumerate(zip(sources, copies))
    ]
    for move in moves:
        move.start()
    keys, w_gate, w_up, values, w_down = copies
    moves[0].wait()
    moves[1].wait()
    k = keys[...]
    g = nn(k, w_gate[...])
    gate[...] = g
    moves[2].wait()
    u = nn(k, w_up[...])
    up[...] = u
    act, slope, _ = silu_parts(g)
    mix = (act * u).astype(BF)
    mixed[...] = mix
    moves[3].wait()
    t = (-as_column(rates[...]) * values[...].astype(F32)).astype(BF)
    target[...] = t
    whole[:, 2 * DH :] = tn(mix, t)
    sent = [send_part(whole, terms, out_sems, 2)]
    moves[4].wait()
    m = nt(t, w_down[...])
    mid[...] = m
    dg = (m * u * slope).astype(BF)
    du = (m * act).astype(BF)
    dgate[...] = dg
    dup[...] = du
    whole[:, :DH] = tn(k, dg)
    sent.append(send_part(whole, terms, out_sems, 0))
    whole[:, DH : 2 * DH] = tn(k, du)
    sent.append(send_part(whole, terms, out_sems, 1))
    for copy in sent:
        copy.wait()


def query_forward(new, queries, cotangent, gain, stats, output, act_out, slope_out, mixed):
    q = queries[...]
    g = nn(q, new[0])
    u = nn(q, new[1])
    act, slope, _ = silu_parts(g)
    mix = (act * u).astype(BF)
    out = nn(mix, new[2])
    squares = jnp.sum(out * out, axis=1, keepdims=True)
    aligned = jnp.sum(cotangent[...].astype(F32) * gain[...] * out, axis=1, keepdims=True)
    lane = lax.broadcasted_iota(jnp.int32, stats.shape, 1)
    stats[...] = jnp.where(lane == 0, squares, aligned)
    output[...] = out
    act_out[...] = act
    slope_out[...] = u * slope
    mixed[...] = mix


def query_backward_body(
    new, queries, cotangent, gain, stats, other, output, act, slope, mixed, *refs
):
    terms, query_grad, whole, sems = refs
    both = stats[...] + other[...]
    inverse_rms = lax.rsqrt(both[:, :1] / (2 * DH) + 1e-05)
    aligned = both[:, 1:2]
    grad_output = (
        gain[...] * cotangent[...].astype(F32) * inverse_rms
        - output[...] * (aligned * inverse_rms * inverse_rms * inverse_rms / (2 * DH))
    ).astype(BF)
    whole[:, 2 * DH :] = tn(mixed[...], grad_output)
    sent = [send_part(whole, terms, sems, 2)]
    mid = nt(grad_output, new[2])
    dg = (mid * slope[...]).astype(BF)
    du = (mid * act[...]).astype(BF)
    q = queries[...]
    whole[:, :DH] = tn(q, dg)
    sent.append(send_part(whole, terms, sems, 0))
    whole[:, DH : 2 * DH] = tn(q, du)
    sent.append(send_part(whole, terms, sems, 1))
    query_grad[...] = (nt(dg, new[0]) + nt(du, new[1])).astype(BF)
    for copy in sent:
        copy.wait()


def key_backward(
    cots, w_gate, w_up, w_down, rates, keys, stored, terms, key_grad, value_grad, whole, sems
):
    gate, up, mid, mixed, target, dgate, dup = stored
    k = keys[...]
    t = target[...]
    back_gate = nn(k, cots[0])
    back_up = nn(k, cots[1])
    back_mixed = nt(t, cots[2])
    g = gate[...]
    u = up[...]
    m = mid[...]
    act, slope, sigma = silu_parts(g)
    curve = sigma * (1.0 - sigma) * (2.0 + g * (1.0 - 2.0 * sigma))
    bm = (back_gate * u * slope + back_up * act).astype(BF)
    whole[:, 2 * DH :] = tn(bm, t)
    sent = [send_part(whole, terms, sems, 2)]
    ub = (back_gate * m * slope + back_mixed * act).astype(BF)
    whole[:, DH : 2 * DH] = tn(k, ub)
    sent.append(send_part(whole, terms, sems, 1))
    gb = (back_gate * m * u * curve + back_up * m * slope + back_mixed * u * slope).astype(BF)
    whole[:, :DH] = tn(k, gb)
    sent.append(send_part(whole, terms, sems, 0))
    key_grad[...] = (
        nt(dgate[...], cots[0])
        + nt(dup[...], cots[1])
        + nt(gb, w_gate[...])
        + nt(ub, w_up[...])
    ).astype(BF)
    value_sum = nn(mixed[...], cots[2]) + nn(bm, w_down[...])
    value_grad[...] = (-as_column(rates[...]) * value_sum).astype(BF)
    for copy in sent:
        copy.wait()


def share_body(share, pieces, out_a, out_b, out_c, total):
    step = pl.program_id(0)

    @pl.when(step == 0)
    def _():
        total[...] = share[...]

    total[...] += jnp.sum(pieces[...], axis=0)

    @pl.when(step == SUM_STEPS - 1)
    def _():
        out_a[0] = total[:, :DH]
        out_b[0] = total[:, DH : 2 * DH]
        out_c[0] = total[:, 2 * DH :]


def weight_shares(share, pieces):
    out = pl.BlockSpec((1, 8, DH), lambda i: (0, 0, 0))
    return pl.pallas_call(
        share_body,
        grid=(SUM_STEPS,),
        in_specs=[
            pl.BlockSpec((8, WIDE), lambda i: (0, 0)),
            pieces_spec(pieces),
        ],
        out_specs=[out] * 3,
        out_shape=[shape(1, 8, DH)] * 3,
        scratch_shapes=[pltpu.VMEM((8, WIDE), F32)],
        compiler_params=pltpu.CompilerParams(vmem_limit_bytes=VMEM_BYTES),
    )(share, pieces)


def ortho_body(own, a, b, c, d, w_gate, w_up, w_down, queries, cotangent, gain, *refs):
    new, kept, norm, query_refs, (current, gram) = refs[0], refs[1], refs[2], refs[3:8], refs[8:]
    place_rows(own, (a, b, c, d), current)
    for i in EACH:
        matrix = current[i]
        root = jnp.sqrt(jnp.sum(matrix * matrix, keepdims=True) + 1e-06)
        norm[i] = jnp.broadcast_to(root, norm.shape[1:])
        unit = matrix * (1.0 / root)
        current[i] = unit
        kept[i, 0] = unit.astype(BF)
    for step in range(NS_STEPS):
        for i in EACH:
            narrow = kept[i, 3 * step]
            square = nt(narrow, narrow)
            gram[i] = square
            kept[i, 3 * step + 1] = square.astype(BF)
        for i in EACH:
            low = kept[i, 3 * step + 1]
            kept[i, 3 * step + 2] = (coef_second * gram[i] + coef_third * nn(low, low)).astype(BF)
        for i, weight in enumerate((w_gate, w_up, w_down)):
            later = coef_first * current[i] + nn(kept[i, 3 * step + 2], kept[i, 3 * step])
            if step < NS_STEPS - 1:
                current[i] = later
                kept[i, 3 * step + 3] = later.astype(BF)
            else:
                new[i] = (weight[...].astype(F32) - inner_step * later).astype(BF)
    query_forward(new, queries, cotangent, gain, *query_refs)


def ortho_back_body(
    own, a, b, c, d, kept, norm, w_gate, w_up, w_down, rates, keys, *refs
):
    stored, (terms, key_grad, value_grad) = refs[:7], refs[7:10]
    cots, grad, grad_low, half, sym, whole, sems = refs[10:]
    place_rows(own, (a, b, c, d), grad)
    for i in EACH:
        start = grad[i] * (-inner_step)
        grad[i] = start
        grad_low[i] = start.astype(BF)
    for step in reversed(range(NS_STEPS)):
        for i in EACH:
            half[i] = nt(grad_low[i], kept[i, 3 * step])
        for i in EACH:
            both = half[i] + jnp.transpose(half[i])
            sym[i] = both.astype(BF)
        for i in EACH:
            half[i] = coef_third * nn(sym[i], kept[i, 3 * step + 1])
        for i in EACH:
            full = coef_second * sym[i].astype(F32) + (half[i] + jnp.transpose(half[i]))
            sym[i] = full.astype(BF)
        for i in EACH:
            later = (
                coef_first * grad[i]
                + nn(kept[i, 3 * step + 2], grad_low[i])
                + nn(sym[i], kept[i, 3 * step])
            )
            grad[i] = later
            if step > 0:
                grad_low[i] = later.astype(BF)
    for i in EACH:
        unit = kept[i, 0].astype(F32)
        along = jnp.sum(grad[i] * unit, keepdims=True)
        cots[i] = ((grad[i] - unit * along) * (1.0 / norm[i, :1, :1])).astype(BF)
    key_backward(
        cots, w_gate, w_up, w_down, rates, keys, stored, terms, key_grad, value_grad, whole, sems
    )


def local(queries, key_rows, value_rows, step_rates, w_gate, w_up, w_down, out_gain, cotangent):
    tokens = queries.shape[1]
    queries, key_rows, value_rows, cotangent = (
        a[0] for a in (queries, key_rows, value_rows, cotangent)
    )
    w_gate, w_up, w_down = w_gate[0], w_up[0], w_down[0]
    own = own_table()

    whole = pltpu.VMEM((DH, WIDE), F32)
    out_sems = pltpu.SemaphoreType.DMA((3,))
    wide = shape(tokens, DH)
    low = shape(tokens, DH, dtype=BF)
    three = shape(3, DH, DH, dtype=BF)
    three_f32 = pltpu.VMEM((3, DH, DH), F32)
    three_low = pltpu.VMEM((3, DH, DH), BF)
    token_low = pltpu.VMEM((tokens, DH), BF)
    square_low = pltpu.VMEM((DH, DH), BF)
    terms, *stored = call(
        key_body,
        [shape(DH, WIDE), wide, wide, wide, low, low, low, low],
        step_rates,
        key_rows,
        w_gate,
        w_up,
        value_rows,
        w_down,
        scratch=[
            whole,
            token_low,
            square_low,
            square_low,
            token_low,
            square_low,
            pltpu.SemaphoreType.DMA((5,)),
            out_sems,
        ],
        specs=[VMEM] + [HBM] * 5,
        out_specs=[HBM] + [VMEM] * 7,
    )
    blocks, _ = sum_everywhere(terms)
    new, kept, norm, stats, *query_stored = call(
        ortho_body,
        [
            three,
            shape(3, 9, DH, DH, dtype=BF),
            shape(3, 8, 128),
            shape(tokens, 128),
            wide,
            wide,
            wide,
            low,
        ],
        *blocks,
        w_gate,
        w_up,
        w_down,
        queries,
        cotangent,
        out_gain,
        scalars=own,
        scratch=[three_f32, three_f32],
    )
    other = lax.ppermute(stats, ALL, OTHER_CORE)
    terms, query_grad = call(
        query_backward_body,
        [shape(DH, WIDE), low],
        new,
        queries,
        cotangent,
        out_gain,
        stats,
        other,
        *query_stored,
        scratch=[whole, out_sems],
        out_specs=[HBM, VMEM],
    )
    blocks, share = sum_everywhere(terms)
    terms, key_grad, value_grad = call(
        ortho_back_body,
        [shape(DH, WIDE), low, low],
        *blocks,
        kept,
        norm,
        w_gate,
        w_up,
        w_down,
        step_rates,
        key_rows,
        *stored,
        scalars=own,
        scratch=[three_low, three_f32, three_low, three_f32, three_low, whole, out_sems],
        out_specs=[HBM, VMEM, VMEM],
    )
    grads = weight_shares(share, to_owners(terms))
    return (query_grad[None], key_grad[None], value_grad[None], *grads)


def solution(mesh):
    split = Mesh(
        mesh.devices.reshape(4, 4, 4, mesh.shape["head"]), ("tok_0", "tok_1", "tok_2", "head")
    )
    rows = P("head", TOK, None)
    weight = P("head", None, None)
    in_specs = (
        rows,
        rows,
        rows,
        P("head", TOK),
        weight,
        weight,
        weight,
        P("head", None),
        rows,
    )
    return jax.shard_map(
        local, mesh=split, in_specs=in_specs, out_specs=(rows,) * 6, check_vma=False
    )
```

```python
import jax
import jax.numpy as jnp
from jax import lax
from jax.experimental import pallas as pl
from jax.experimental.pallas import tpu as pltpu
from jax.sharding import Mesh
from jax.sharding import PartitionSpec as P

TOK = ("tok_0", "tok_1", "tok_2")
ALL = TOK + ("head",)
NS_STEPS = 3
DH = 512
WIDE = 3 * DH
BF = jnp.bfloat16
F32 = jnp.float32
coef_first = 3.4445
coef_second = -4.775
coef_third = 2.0315
inner_step = 0.5
VMEM_BYTES = 24 * 1024 * 1024


def flat_at(x, y, z, c):
    return ((x * 4 + y) * 4 + z) * 2 + c


def links(move):
    out = []
    for x in range(4):
        for y in range(4):
            for z in range(4):
                for c in range(2):
                    out.append((flat_at(x, y, z, c), flat_at(*move(x, y, z, c))))
    return out


def pair(i, near):
    return i ^ 1 if near else 3 - i


def partner_links(level, step):
    axis = 3 - step

    def move(x, y, z, c):
        at = [x, y, z]
        at[axis] = pair(at[axis], (level == 1) != (c == 1))
        return (*at, c)

    return links(move)


def antipode_links(step):
    flip = {1: lambda i: 3 - i, 2: lambda i: i ^ 1, 3: lambda i: i ^ 2}[step]
    return links(lambda x, y, z, c: (flip(x), flip(y), flip(z), c))


PARTNERS = {(level, step): partner_links(level, step) for level in (1, 2) for step in (1, 2, 3)}
PARTNERS.update({(3, step): antipode_links(step) for step in (1, 2, 3)})
OTHER_CORE = links(lambda x, y, z, c: (x, y, z, 1 - c))


def colour(x, y, z, low):
    code = 0
    for at in (x, y, z):
        code = 2 * code + (((at + 1) // 2) % 2 if low else at // 2)
    return min(code, 7 - code)


PLACES = [(x, y, z) for x in range(4) for y in range(4) for z in range(4)]


def of_colour(wanted, c):
    return [t for t, at in enumerate(PLACES) if colour(*at, c == 0) == wanted]


COLOUR_GROUPS = [[2 * t + c for t in of_colour(q, c)] for c in range(2) for q in range(4)]
TABLE = [
    [
        [colour(*at, c == 0), colour(*at, c == 1), t]
        + [t for q in range(4) for t in of_colour(q, c)]
        for c in range(2)
    ]
    for t, at in enumerate(PLACES)
]


def own_table():
    table = jnp.asarray(TABLE, jnp.int32)
    return table[lax.axis_index(TOK), lax.axis_index("head")]


SMEM = pl.BlockSpec(memory_space=pltpu.SMEM)
VMEM = pl.BlockSpec(memory_space=pltpu.VMEM)
HBM = pl.BlockSpec(memory_space=pltpu.HBM)


def call(body, outs, *args, scratch=(), scalars=None, flops=0, specs=None, out_specs=None, limit=VMEM_BYTES):
    specs = specs or [VMEM] * len(args)
    if scalars is not None:
        specs = [SMEM] + specs
        args = (scalars, *args)
    moved = sum(a.size * a.dtype.itemsize for a in args) + sum(
        o.size * o.dtype.itemsize for o in outs
    )
    return pl.pallas_call(
        body,
        out_shape=list(outs),
        in_specs=specs,
        out_specs=out_specs or [VMEM] * len(outs),
        scratch_shapes=list(scratch),
        compiler_params=pltpu.CompilerParams(vmem_limit_bytes=limit),
        cost_estimate=pl.CostEstimate(flops=flops, bytes_accessed=moved, transcendentals=0),
    )(*args)


def shape(*dims, dtype=F32):
    return jax.ShapeDtypeStruct(dims, dtype)


def nn(a, b):
    return jnp.dot(a, b, preferred_element_type=F32)


def nt(a, b):
    return lax.dot_general(a, b, (((1,), (1,)), ((), ())), preferred_element_type=F32)


def tn(a, b):
    return lax.dot_general(a, b, (((0,), (0,)), ((), ())), preferred_element_type=F32)


def rows_at(index, rows):
    return pl.ds(pl.multiple_of(index * rows, rows), rows)


def hand_out(own, whole, outs, rows):
    for step in range(4):
        outs[step][...] = whole[rows_at(own ^ step, rows), :]


def columns(index):
    return slice(index * DH, (index + 1) * DH)


def fold_body(own, a, b, c, d, *outs):
    rows = outs[0].shape[0]
    for step in range(4):
        at = rows_at(own[1] ^ step, rows)
        outs[step][...] = (a[at, :] + b[at, :]) + (c[at, :] + d[at, :])


def total_body(*refs):
    *parts, out = refs
    values = [part[...] for part in parts]
    while len(values) > 1:
        values = [values[i] + values[i + 1] for i in range(0, len(values), 2)]
    out[...] = values[0]


def join_body(own, a, b, c, d, out):
    rows = a.shape[0]
    for step, piece in enumerate((a, b, c, d)):
        out[rows_at(own[1] ^ step, rows), :] = piece[...]


def received(blocks, level):
    return [blocks[0]] + [
        lax.ppermute(blocks[step], ALL, PARTNERS[level, step]) for step in (1, 2, 3)
    ]


def with_other(blocks, done):
    return lax.optimization_barrier((tuple(blocks), done))


def sum_everywhere(arrived, own):
    piece_shape = [shape(32, WIDE)]
    blocks = call(fold_body, piece_shape * 4, *arrived, scalars=own)
    (piece,) = call(total_body, piece_shape, *received(blocks, 2))
    (piece,) = call(total_body, piece_shape, *received([piece] * 4, 3))
    (piece,) = call(join_body, [shape(128, WIDE)], *received([piece] * 4, 2), scalars=own)
    return received([piece] * 4, 1)


def silu_parts(pre_gate):
    sigma_gate = jax.nn.sigmoid(pre_gate)
    act_gate = pre_gate * sigma_gate
    slope_gate = sigma_gate * (1.0 + pre_gate * (1.0 - sigma_gate))
    return (act_gate, slope_gate, sigma_gate)


def as_column(row):
    return jnp.transpose(jnp.broadcast_to(row, (128, row.shape[1])))[:, :1]


def key_body(own, *refs):
    sources, outs, finals = refs[:6], refs[6:10], refs[10:17]
    copies, stored, whole, in_sems, out_sems = refs[17:23], refs[23:30], *refs[30:]
    moves = [
        pltpu.make_async_copy(source, copy, in_sems.at[i])
        for i, (source, copy) in enumerate(zip(sources, copies))
    ]
    for move in moves:
        move.start()
    keys, w_gate, w_up, rates, values, w_down = copies
    gate, up, mid, mixed, target, dgate, dup = stored
    sent = []

    def send(source, goal):
        sent.append(pltpu.make_async_copy(source, goal, out_sems.at[len(sent)]))
        sent[-1].start()

    def keep(index, value):
        stored[index][...] = value
        send(stored[index], finals[index])

    def send_quarters(index):
        for step in range(4):
            at = (rows_at(own[0] ^ step, DH // 4), columns(index))
            send(whole.at[at], outs[step].at[:, columns(index)])

    moves[0].wait()
    moves[1].wait()
    k = keys[...]
    g = nn(k, w_gate[...])
    keep(0, g)
    moves[2].wait()
    u = nn(k, w_up[...])
    keep(1, u)
    act, slope, _ = silu_parts(g)
    mix = (act * u).astype(BF)
    keep(3, mix)
    moves[3].wait()
    moves[4].wait()
    t = (-as_column(rates[...]) * values[...].astype(F32)).astype(BF)
    keep(4, t)
    whole[:, columns(2)] = tn(mix, t)
    send_quarters(2)
    moves[5].wait()
    m = nt(t, w_down[...])
    keep(2, m)
    du = (m * act).astype(BF)
    keep(6, du)
    whole[:, columns(1)] = tn(k, du)
    send_quarters(1)
    dg = (m * u * slope).astype(BF)
    keep(5, dg)
    whole[:, columns(0)] = tn(k, dg)
    send_quarters(0)
    for copy in sent:
        copy.wait()


def query_forward(new, queries, cotangent, gain, stats, output, act_out, slope_out, mixed):
    q = queries[...]
    g = nn(q, new[0])
    u = nn(q, new[1])
    act, slope, _ = silu_parts(g)
    mix = (act * u).astype(BF)
    out = nn(mix, new[2])
    squares = jnp.sum(out * out, axis=1, keepdims=True)
    aligned = jnp.sum(cotangent[...].astype(F32) * gain[...] * out, axis=1, keepdims=True)
    lane = lax.broadcasted_iota(jnp.int32, stats.shape, 1)
    stats[...] = jnp.where(lane == 0, squares, aligned)
    output[...] = out
    act_out[...] = act
    slope_out[...] = u * slope
    mixed[...] = mix


def query_terms_body(
    own, w_down, queries, cotangent, gain, stats, other, output, act, slope, mixed, *refs
):
    outs, dgate, dup, whole = refs[:4], refs[4], refs[5], refs[6]
    both = stats[...] + other[...]
    inverse_rms = lax.rsqrt(both[:, :1] / (2 * DH) + 1e-05)
    aligned = both[:, 1:2]
    grad_output = (
        gain[...] * cotangent[...].astype(F32) * inverse_rms
        - output[...] * (aligned * inverse_rms * inverse_rms * inverse_rms / (2 * DH))
    ).astype(BF)
    mid = nt(grad_output, w_down[2])
    dg = (mid * slope[...]).astype(BF)
    du = (mid * act[...]).astype(BF)
    dgate[...] = dg
    dup[...] = du
    q = queries[...]
    whole[:, 2 * DH :] = tn(mixed[...], grad_output)
    whole[:, :DH] = tn(q, dg)
    whole[:, DH : 2 * DH] = tn(q, du)
    hand_out(own[0], whole, outs, DH // 4)


def query_grad_body(new, dgate, dup, query_grad):
    query_grad[...] = (nt(dgate[...], new[0]) + nt(dup[...], new[1])).astype(BF)


def key_terms(cots, keys, gate, up, mid, target, back_mid, gate_back, up_back, terms):
    k = keys[...]
    t = target[...]
    back_gate = nn(k, cots[0])
    back_up = nn(k, cots[1])
    back_mixed = nt(t, cots[2])
    g = gate[...]
    u = up[...]
    m = mid[...]
    act, slope, sigma = silu_parts(g)
    curve = sigma * (1.0 - sigma) * (2.0 + g * (1.0 - 2.0 * sigma))
    bm = (back_gate * u * slope + back_up * act).astype(BF)
    gb = (back_gate * m * u * curve + back_up * m * slope + back_mixed * u * slope).astype(BF)
    ub = (back_gate * m * slope + back_mixed * act).astype(BF)
    back_mid[...] = bm
    gate_back[...] = gb
    up_back[...] = ub
    terms[:, :DH] = tn(k, gb)
    terms[:, DH : 2 * DH] = tn(k, ub)
    terms[:, 2 * DH :] = tn(bm, t)


def key_grads_body(
    cots, w_gate, w_up, w_down, rates, mixed, dgate, dup, back_mid, gate_back, up_back, *outs
):
    key_grad, value_grad = outs
    key_grad[...] = (
        nt(dgate[...], cots[0])
        + nt(dup[...], cots[1])
        + nt(gate_back[...], w_gate[...])
        + nt(up_back[...], w_up[...])
    ).astype(BF)
    value_sum = nn(mixed[...], cots[2]) + nn(back_mid[...], w_down[...])
    value_grad[...] = (-as_column(rates[...]) * value_sum).astype(BF)


def share_body(share, pieces, out_a, out_b, out_c):
    value = share[...] + jnp.sum(pieces[...], axis=0)
    for index, out in enumerate((out_a, out_b, out_c)):
        out[0] = value[:, columns(index)]


EACH = range(3)


def ortho_body(own, a, b, c, d, w_gate, w_up, w_down, queries, cotangent, gain, *refs):
    new, kept, norm, query_refs, (current, gram) = refs[0], refs[1], refs[2], refs[3:8], refs[8:]
    for step, block in enumerate((a, b, c, d)):
        for i in EACH:
            current[i, rows_at(own[0] ^ step, DH // 4), :] = block[:, columns(i)]
    for i in EACH:
        matrix = current[i]
        root = jnp.sqrt(jnp.sum(matrix * matrix, keepdims=True) + 1e-06)
        norm[i] = jnp.broadcast_to(root, norm.shape[1:])
        unit = matrix * (1.0 / root)
        current[i] = unit
        kept[i, 0] = unit.astype(BF)
    for step in range(NS_STEPS):
        for i in EACH:
            narrow = kept[i, 3 * step]
            square = nt(narrow, narrow)
            gram[i] = square
            kept[i, 3 * step + 1] = square.astype(BF)
        for i in EACH:
            low = kept[i, 3 * step + 1]
            kept[i, 3 * step + 2] = (coef_second * gram[i] + coef_third * nn(low, low)).astype(BF)
        for i, weight in enumerate((w_gate, w_up, w_down)):
            later = coef_first * current[i] + nn(kept[i, 3 * step + 2], kept[i, 3 * step])
            if step < NS_STEPS - 1:
                current[i] = later
                kept[i, 3 * step + 3] = later.astype(BF)
            else:
                new[i] = (weight[...].astype(F32) - inner_step * later).astype(BF)
    query_forward(new, queries, cotangent, gain, *query_refs)


def ortho_back_body(own, a, b, c, d, kept, norm, keys, gate, up, mid, target, *refs):
    cots, share, outs, key_refs = refs[0], refs[1], refs[2:6], refs[6:9]
    grad, grad_low, half, sym, terms = refs[9:]
    for step, block in enumerate((a, b, c, d)):
        for i in EACH:
            grad[i, rows_at(own[0] ^ step, DH // 4), :] = block[:, columns(i)]
    for i in EACH:
        share[:, columns(i)] = grad[i, rows_at(own[2], 8), :]
        start = grad[i] * (-inner_step)
        grad[i] = start
        grad_low[i] = start.astype(BF)
    for step in reversed(range(NS_STEPS)):
        for i in EACH:
            half[i] = nt(grad_low[i], kept[i, 3 * step])
        for i in EACH:
            both = half[i] + jnp.transpose(half[i])
            sym[i] = both.astype(BF)
        for i in EACH:
            half[i] = coef_third * nn(sym[i], kept[i, 3 * step + 1])
        for i in EACH:
            full = coef_second * sym[i].astype(F32) + (half[i] + jnp.transpose(half[i]))
            sym[i] = full.astype(BF)
        for i in EACH:
            later = (
                coef_first * grad[i]
                + nn(kept[i, 3 * step + 2], grad_low[i])
                + nn(sym[i], kept[i, 3 * step])
            )
            grad[i] = later
            if step > 0:
                grad_low[i] = later.astype(BF)
    for i in EACH:
        unit = kept[i, 0].astype(F32)
        along = jnp.sum(grad[i] * unit, keepdims=True)
        cots[i] = ((grad[i] - unit * along) * (1.0 / norm[i, :1, :1])).astype(BF)
    key_terms(cots, keys, gate, up, mid, target, *key_refs, terms)
    for step in range(4):
        first = 3 + 16 * (own[0] ^ step)
        for j in range(16):
            outs[step][8 * j : 8 * j + 8, :] = terms[rows_at(own[first + j], 8), :]


def local(queries, key_rows, value_rows, step_rates, w_gate, w_up, w_down, out_gain, cotangent):
    tokens = queries.shape[1]
    queries, key_rows, value_rows, cotangent = (
        a[0] for a in (queries, key_rows, value_rows, cotangent)
    )
    w_gate, w_up, w_down = w_gate[0], w_up[0], w_down[0]
    own = own_table()

    whole = pltpu.VMEM((DH, WIDE), F32)
    quarters = [shape(DH // 4, WIDE)] * 4
    wide = shape(tokens, DH)
    low = shape(tokens, DH, dtype=BF)
    three = shape(3, DH, DH, dtype=BF)
    three_f32 = pltpu.VMEM((3, DH, DH), F32)
    three_low = pltpu.VMEM((3, DH, DH), BF)
    key_inputs = (key_rows, w_gate, w_up, step_rates, value_rows, w_down)
    stored_shapes = [wide, wide, wide, low, low, low, low]
    *blocks, gate, up, mid, mixed, target, dgate, dup = call(
        key_body,
        [*quarters, *stored_shapes],
        *key_inputs,
        scratch=[
            *(pltpu.VMEM(a.shape, a.dtype) for a in (*key_inputs, *stored_shapes)),
            whole,
            pltpu.SemaphoreType.DMA((6,)),
            pltpu.SemaphoreType.DMA((19,)),
        ],
        scalars=own,
        specs=[HBM] * 6,
        out_specs=[HBM] * 11,
        limit=56 * 1024 * 1024,
    )
    new, kept, norm, stats, *query_stored = call(
        ortho_body,
        [
            three,
            shape(3, 9, DH, DH, dtype=BF),
            shape(3, 8, 128),
            shape(tokens, 128),
            wide,
            wide,
            wide,
            low,
        ],
        *sum_everywhere(received(blocks, 1), own),
        w_gate,
        w_up,
        w_down,
        queries,
        cotangent,
        out_gain,
        scalars=own,
        scratch=[three_f32, three_f32],
    )
    other = lax.ppermute(stats, ALL, OTHER_CORE)
    *blocks, query_dgate, query_dup = call(
        query_terms_body,
        [*quarters, low, low],
        new,
        queries,
        cotangent,
        out_gain,
        stats,
        other,
        *query_stored,
        scratch=[whole],
        scalars=own,
    )
    query_grad = call(
        query_grad_body, [low], new, query_dgate, query_dup, flops=4 * tokens * DH * DH
    )
    blocks, (query_grad,) = with_other(received(blocks, 1), query_grad)
    cots, share, *blocks, back_mid, gate_back, up_back = call(
        ortho_back_body,
        [three, shape(8, WIDE), *quarters, low, low, low],
        *sum_everywhere(blocks, own),
        kept,
        norm,
        key_rows,
        gate,
        up,
        mid,
        target,
        scalars=own,
        scratch=[three_f32, three_low, three_f32, three_low, whole],
    )
    key_grads = call(
        key_grads_body,
        [low, low],
        cots,
        w_gate,
        w_up,
        w_down,
        step_rates,
        mixed,
        dgate,
        dup,
        back_mid,
        gate_back,
        up_back,
        flops=12 * tokens * DH * DH,
    )
    blocks, (key_grad, value_grad) = with_other(received(blocks, 1), key_grads)
    (quarter,) = call(total_body, quarters[:1], *blocks)
    pieces = lax.all_to_all(
        quarter.reshape(16, 8, WIDE), ALL, 0, 0, axis_index_groups=COLOUR_GROUPS, tiled=True
    )
    grads = call(share_body, [shape(1, 8, DH)] * 3, share, pieces)
    return (query_grad[None], key_grad[None], value_grad[None], *grads)


def solution(mesh):
    split = Mesh(
        mesh.devices.reshape(4, 4, 4, mesh.shape["head"]), ("tok_0", "tok_1", "tok_2", "head")
    )
    rows = P("head", TOK, None)
    weight = P("head", None, None)
    in_specs = (
        rows,
        rows,
        rows,
        P("head", TOK),
        weight,
        weight,
        weight,
        P("head", None),
        rows,
    )
    return jax.shard_map(
        local, mesh=split, in_specs=in_specs, out_specs=(rows,) * 6, check_vma=False
    )
```

```python
import jax
import jax.numpy as jnp
from jax import lax
from jax.experimental import pallas as pl
from jax.experimental.pallas import tpu as pltpu
from jax.sharding import Mesh
from jax.sharding import PartitionSpec as P

TOK = ("tok_0", "tok_1", "tok_2")
ALL = TOK + ("head",)
NS_STEPS = 3
DH = 512
WIDE = 3 * DH
BF = jnp.bfloat16
F32 = jnp.float32
coef_first = 3.4445
coef_second = -4.775
coef_third = 2.0315
inner_step = 0.5
VMEM_BYTES = 24 * 1024 * 1024


def flat_at(x, y, z, c):
    return ((x * 4 + y) * 4 + z) * 2 + c


def links(move):
    out = []
    for x in range(4):
        for y in range(4):
            for z in range(4):
                for c in range(2):
                    out.append((flat_at(x, y, z, c), flat_at(*move(x, y, z, c))))
    return out


def pair(i, near):
    return i ^ 1 if near else 3 - i


def partner_links(level, step):
    axis = 3 - step

    def move(x, y, z, c):
        at = [x, y, z]
        at[axis] = pair(at[axis], (level == 1) != (c == 1))
        return (*at, c)

    return links(move)


def antipode_links(step):
    flip = {1: lambda i: 3 - i, 2: lambda i: i ^ 1, 3: lambda i: i ^ 2}[step]
    return links(lambda x, y, z, c: (flip(x), flip(y), flip(z), c))


PARTNERS = {(level, step): partner_links(level, step) for level in (1, 2) for step in (1, 2, 3)}
PARTNERS.update({(3, step): antipode_links(step) for step in (1, 2, 3)})
OTHER_CORE = links(lambda x, y, z, c: (x, y, z, 1 - c))


def colour(x, y, z, low):
    code = 0
    for at in (x, y, z):
        code = 2 * code + (((at + 1) // 2) % 2 if low else at // 2)
    return min(code, 7 - code)


PLACES = [(x, y, z) for x in range(4) for y in range(4) for z in range(4)]


def of_colour(wanted, c):
    return [t for t, at in enumerate(PLACES) if colour(*at, c == 0) == wanted]


COLOUR_GROUPS = [[2 * t + c for t in of_colour(q, c)] for c in range(2) for q in range(4)]
TOKENS_BY_COLOUR = [[t for q in range(4) for t in of_colour(q, c)] for c in range(2)]


def position():
    return [lax.axis_index(a) for a in TOK], lax.axis_index("head")


def own_colour(near):
    at, core = position()
    low, high = 0, 0
    for i in at:
        low = 2 * low + (((i + 1) >> 1) & 1)
        high = 2 * high + (i >> 1)
    code = jnp.where((core == 0) == near, low, high)
    return jnp.where(code >= 4, 7 - code, code)


def own_index():
    (x, y, z), _ = position()
    return (x * 4 + y) * 4 + z


SMEM = pl.BlockSpec(memory_space=pltpu.SMEM)
VMEM = pl.BlockSpec(memory_space=pltpu.VMEM)
HBM = pl.BlockSpec(memory_space=pltpu.HBM)


def call(body, outs, *args, scratch=(), scalars=None, flops=0, specs=None, out_specs=None, limit=VMEM_BYTES):
    specs = specs or [VMEM] * len(args)
    if scalars is not None:
        specs = [SMEM] + specs
        args = (scalars, *args)
    moved = sum(a.size * a.dtype.itemsize for a in args) + sum(
        o.size * o.dtype.itemsize for o in outs
    )
    return pl.pallas_call(
        body,
        out_shape=list(outs),
        in_specs=specs,
        out_specs=out_specs or [VMEM] * len(outs),
        scratch_shapes=list(scratch),
        compiler_params=pltpu.CompilerParams(vmem_limit_bytes=limit),
        cost_estimate=pl.CostEstimate(flops=flops, bytes_accessed=moved, transcendentals=0),
    )(*args)


def shape(*dims, dtype=F32):
    return jax.ShapeDtypeStruct(dims, dtype)


def nn(a, b):
    return jnp.dot(a, b, preferred_element_type=F32)


def nt(a, b):
    return lax.dot_general(a, b, (((1,), (1,)), ((), ())), preferred_element_type=F32)


def tn(a, b):
    return lax.dot_general(a, b, (((0,), (0,)), ((), ())), preferred_element_type=F32)


def rows_at(index, rows):
    return pl.ds(pl.multiple_of(index * rows, rows), rows)


def hand_out(own, whole, outs, rows):
    for step in range(4):
        outs[step][...] = whole[rows_at(own ^ step, rows), :]


def columns(index):
    return slice(index * DH, (index + 1) * DH)


def fold_body(a, b, c, d, *outs):
    rows = outs[0].shape[0]
    own = own_colour(False)
    for step in range(4):
        at = rows_at(own ^ step, rows)
        outs[step][...] = (a[at, :] + b[at, :]) + (c[at, :] + d[at, :])


def total_body(*refs):
    *parts, out = refs
    values = [part[...] for part in parts]
    while len(values) > 1:
        values = [values[i] + values[i + 1] for i in range(0, len(values), 2)]
    out[...] = values[0]


def join_body(a, b, c, d, out):
    rows = a.shape[0]
    own = own_colour(False)
    for step, piece in enumerate((a, b, c, d)):
        out[rows_at(own ^ step, rows), :] = piece[...]


def received(blocks, level):
    return [blocks[0]] + [
        lax.ppermute(blocks[step], ALL, PARTNERS[level, step]) for step in (1, 2, 3)
    ]


def with_other(blocks, done):
    return lax.optimization_barrier((tuple(blocks), done))


def sum_everywhere(arrived):
    piece_shape = [shape(32, WIDE)]
    blocks = call(fold_body, piece_shape * 4, *arrived)
    (piece,) = call(total_body, piece_shape, *received(blocks, 2))
    (piece,) = call(total_body, piece_shape, *received([piece] * 4, 3))
    (piece,) = call(join_body, [shape(128, WIDE)], *received([piece] * 4, 2))
    return received([piece] * 4, 1)


def silu_parts(pre_gate):
    sigma_gate = jax.nn.sigmoid(pre_gate)
    act_gate = pre_gate * sigma_gate
    slope_gate = sigma_gate * (1.0 + pre_gate * (1.0 - sigma_gate))
    return (act_gate, slope_gate, sigma_gate)


def as_column(row):
    return jnp.transpose(jnp.broadcast_to(row, (128, row.shape[1])))[:, :1]


def key_body(*refs):
    sources, outs, finals = refs[:6], refs[6:10], refs[10:17]
    copies, stored, whole, in_sems, out_sems = refs[17:23], refs[23:30], *refs[30:]
    moves = [
        pltpu.make_async_copy(source, copy, in_sems.at[i])
        for i, (source, copy) in enumerate(zip(sources, copies))
    ]
    for move in moves:
        move.start()
    keys, w_gate, w_up, rates, values, w_down = copies
    gate, up, mid, mixed, target, dgate, dup = stored
    sent = []
    own = own_colour(True)

    def send(source, goal):
        sent.append(pltpu.make_async_copy(source, goal, out_sems.at[len(sent)]))
        sent[-1].start()

    def keep(index, value):
        stored[index][...] = value
        send(stored[index], finals[index])

    def send_quarters(index):
        for step in range(4):
            at = (rows_at(own ^ step, DH // 4), columns(index))
            send(whole.at[at], outs[step].at[:, columns(index)])

    moves[0].wait()
    moves[1].wait()
    k = keys[...]
    g = nn(k, w_gate[...])
    keep(0, g)
    moves[2].wait()
    u = nn(k, w_up[...])
    keep(1, u)
    act, slope, _ = silu_parts(g)
    mix = (act * u).astype(BF)
    keep(3, mix)
    moves[3].wait()
    moves[4].wait()
    t = (-as_column(rates[...]) * values[...].astype(F32)).astype(BF)
    keep(4, t)
    whole[:, columns(2)] = tn(mix, t)
    send_quarters(2)
    moves[5].wait()
    m = nt(t, w_down[...])
    keep(2, m)
    du = (m * act).astype(BF)
    keep(6, du)
    whole[:, columns(1)] = tn(k, du)
    send_quarters(1)
    dg = (m * u * slope).astype(BF)
    keep(5, dg)
    whole[:, columns(0)] = tn(k, dg)
    send_quarters(0)
    for copy in sent:
        copy.wait()


def query_forward(new, queries, cotangent, gain, stats, output, act_out, slope_out, mixed):
    q = queries[...]
    g = nn(q, new[0])
    u = nn(q, new[1])
    act, slope, _ = silu_parts(g)
    mix = (act * u).astype(BF)
    out = nn(mix, new[2])
    squares = jnp.sum(out * out, axis=1, keepdims=True)
    aligned = jnp.sum(cotangent[...].astype(F32) * gain[...] * out, axis=1, keepdims=True)
    lane = lax.broadcasted_iota(jnp.int32, stats.shape, 1)
    stats[...] = jnp.where(lane == 0, squares, aligned)
    output[...] = out
    act_out[...] = act
    slope_out[...] = u * slope
    mixed[...] = mix


def query_terms_body(
    w_down, queries, cotangent, gain, stats, other, output, act, slope, mixed, *refs
):
    outs, dgate, dup, whole = refs[:4], refs[4], refs[5], refs[6]
    both = stats[...] + other[...]
    inverse_rms = lax.rsqrt(both[:, :1] / (2 * DH) + 1e-05)
    aligned = both[:, 1:2]
    grad_output = (
        gain[...] * cotangent[...].astype(F32) * inverse_rms
        - output[...] * (aligned * inverse_rms * inverse_rms * inverse_rms / (2 * DH))
    ).astype(BF)
    mid = nt(grad_output, w_down[2])
    dg = (mid * slope[...]).astype(BF)
    du = (mid * act[...]).astype(BF)
    dgate[...] = dg
    dup[...] = du
    q = queries[...]
    whole[:, 2 * DH :] = tn(mixed[...], grad_output)
    whole[:, :DH] = tn(q, dg)
    whole[:, DH : 2 * DH] = tn(q, du)
    hand_out(own_colour(True), whole, outs, DH // 4)


def query_grad_body(new, dgate, dup, query_grad):
    query_grad[...] = (nt(dgate[...], new[0]) + nt(dup[...], new[1])).astype(BF)


def key_terms(cots, keys, gate, up, mid, target, back_mid, gate_back, up_back, terms):
    k = keys[...]
    t = target[...]
    back_gate = nn(k, cots[0])
    back_up = nn(k, cots[1])
    back_mixed = nt(t, cots[2])
    g = gate[...]
    u = up[...]
    m = mid[...]
    act, slope, sigma = silu_parts(g)
    curve = sigma * (1.0 - sigma) * (2.0 + g * (1.0 - 2.0 * sigma))
    bm = (back_gate * u * slope + back_up * act).astype(BF)
    gb = (back_gate * m * u * curve + back_up * m * slope + back_mixed * u * slope).astype(BF)
    ub = (back_gate * m * slope + back_mixed * act).astype(BF)
    back_mid[...] = bm
    gate_back[...] = gb
    up_back[...] = ub
    terms[:, :DH] = tn(k, gb)
    terms[:, DH : 2 * DH] = tn(k, ub)
    terms[:, 2 * DH :] = tn(bm, t)


def key_grads_body(
    cots, w_gate, w_up, w_down, rates, mixed, dgate, dup, back_mid, gate_back, up_back, *outs
):
    key_grad, value_grad = outs
    key_grad[...] = (
        nt(dgate[...], cots[0])
        + nt(dup[...], cots[1])
        + nt(gate_back[...], w_gate[...])
        + nt(up_back[...], w_up[...])
    ).astype(BF)
    value_sum = nn(mixed[...], cots[2]) + nn(back_mid[...], w_down[...])
    value_grad[...] = (-as_column(rates[...]) * value_sum).astype(BF)


def share_body(share, pieces, out_a, out_b, out_c):
    value = share[...] + jnp.sum(pieces[...], axis=0)
    for index, out in enumerate((out_a, out_b, out_c)):
        out[0] = value[:, columns(index)]


EACH = range(3)


HALF = DH // 2


def symmetric_product(ref, product, full, added, low):
    value = ref[...]
    for rows, cols in ((slice(0, HALF), slice(0, DH)), (slice(HALF, DH), slice(HALF, DH))):
        other = value[cols] if product is nt else value[:, cols]
        block = product(value[rows], other)
        if added is not None:
            block = coef_second * added[rows, cols] + coef_third * block
        if full is not None:
            full[rows, cols] = block
        low[rows, cols] = block.astype(BF)
    low[HALF:, :HALF] = jnp.transpose(low[:HALF, HALF:])


def ortho_body(a, b, c, d, w_gate, w_up, w_down, queries, cotangent, gain, *refs):
    new, kept, norm, query_refs, (current, gram) = refs[0], refs[1], refs[2], refs[3:8], refs[8:]
    own = own_colour(True)
    for step, block in enumerate((a, b, c, d)):
        for i in EACH:
            current[i, rows_at(own ^ step, DH // 4), :] = block[:, columns(i)]
    for i in EACH:
        matrix = current[i]
        root = jnp.sqrt(jnp.sum(matrix * matrix, keepdims=True) + 1e-06)
        norm[i] = jnp.broadcast_to(root, norm.shape[1:])
        unit = matrix * (1.0 / root)
        current[i] = unit
        kept[i, 0] = unit.astype(BF)
    for step in range(NS_STEPS):
        for i in EACH:
            symmetric_product(kept.at[i, 3 * step], nt, gram.at[i], None, kept.at[i, 3 * step + 1])
        for i in EACH:
            symmetric_product(kept.at[i, 3 * step + 1], nn, None, gram.at[i], kept.at[i, 3 * step + 2])
        for i, weight in enumerate((w_gate, w_up, w_down)):
            later = coef_first * current[i] + nn(kept[i, 3 * step + 2], kept[i, 3 * step])
            if step < NS_STEPS - 1:
                current[i] = later
                kept[i, 3 * step + 3] = later.astype(BF)
            else:
                new[i] = (weight[...].astype(F32) - inner_step * later).astype(BF)
    query_forward(new, queries, cotangent, gain, *query_refs)


def ortho_back_body(by_colour, a, b, c, d, kept, norm, keys, gate, up, mid, target, *refs):
    cots, share, outs, key_refs = refs[0], refs[1], refs[2:6], refs[6:9]
    grad, grad_low, half, sym, terms = refs[9:]
    near = own_colour(True)
    for step, block in enumerate((a, b, c, d)):
        for i in EACH:
            grad[i, rows_at(near ^ step, DH // 4), :] = block[:, columns(i)]
    for i in EACH:
        share[:, columns(i)] = grad[i, rows_at(own_index(), 8), :]
        start = grad[i] * (-inner_step)
        grad[i] = start
        grad_low[i] = start.astype(BF)
    for step in reversed(range(NS_STEPS)):
        for i in EACH:
            half[i] = nt(grad_low[i], kept[i, 3 * step])
        for i in EACH:
            both = half[i] + jnp.transpose(half[i])
            sym[i] = both.astype(BF)
        for i in EACH:
            half[i] = coef_third * nn(sym[i], kept[i, 3 * step + 1])
        for i in EACH:
            full = coef_second * sym[i].astype(F32) + (half[i] + jnp.transpose(half[i]))
            sym[i] = full.astype(BF)
        for i in EACH:
            later = (
                coef_first * grad[i]
                + nn(kept[i, 3 * step + 2], grad_low[i])
                + nn(sym[i], kept[i, 3 * step])
            )
            grad[i] = later
            if step > 0:
                grad_low[i] = later.astype(BF)
    for i in EACH:
        unit = kept[i, 0].astype(F32)
        along = jnp.sum(grad[i] * unit, keepdims=True)
        cots[i] = ((grad[i] - unit * along) * (1.0 / norm[i, :1, :1])).astype(BF)
    key_terms(cots, keys, gate, up, mid, target, *key_refs, terms)
    for step in range(4):
        first = 16 * (near ^ step)
        for j in range(16):
            outs[step][8 * j : 8 * j + 8, :] = terms[rows_at(by_colour[first + j], 8), :]


def local(queries, key_rows, value_rows, step_rates, w_gate, w_up, w_down, out_gain, cotangent):
    tokens = queries.shape[1]
    queries, key_rows, value_rows, cotangent = (
        a[0] for a in (queries, key_rows, value_rows, cotangent)
    )
    w_gate, w_up, w_down = w_gate[0], w_up[0], w_down[0]
    whole = pltpu.VMEM((DH, WIDE), F32)
    quarters = [shape(DH // 4, WIDE)] * 4
    wide = shape(tokens, DH)
    low = shape(tokens, DH, dtype=BF)
    three = shape(3, DH, DH, dtype=BF)
    three_f32 = pltpu.VMEM((3, DH, DH), F32)
    three_low = pltpu.VMEM((3, DH, DH), BF)
    key_inputs = (key_rows, w_gate, w_up, step_rates, value_rows, w_down)
    stored_shapes = [wide, wide, wide, low, low, low, low]
    *blocks, gate, up, mid, mixed, target, dgate, dup = call(
        key_body,
        [*quarters, *stored_shapes],
        *key_inputs,
        scratch=[
            *(pltpu.VMEM(a.shape, a.dtype) for a in (*key_inputs, *stored_shapes)),
            whole,
            pltpu.SemaphoreType.DMA((6,)),
            pltpu.SemaphoreType.DMA((19,)),
        ],
        specs=[HBM] * 6,
        out_specs=[HBM] * 11,
        limit=56 * 1024 * 1024,
    )
    arrived, (mine,) = with_other(received(blocks, 1), call(total_body, quarters[:1], blocks[0]))
    arrived = (mine, *arrived[1:])
    new, kept, norm, stats, *query_stored = call(
        ortho_body,
        [
            three,
            shape(3, 9, DH, DH, dtype=BF),
            shape(3, 8, 128),
            shape(tokens, 128),
            wide,
            wide,
            wide,
            low,
        ],
        *sum_everywhere(arrived),
        w_gate,
        w_up,
        w_down,
        queries,
        cotangent,
        out_gain,
        scratch=[three_f32, three_f32],
    )
    other = lax.ppermute(stats, ALL, OTHER_CORE)
    *blocks, query_dgate, query_dup = call(
        query_terms_body,
        [*quarters, low, low],
        new,
        queries,
        cotangent,
        out_gain,
        stats,
        other,
        *query_stored,
        scratch=[whole],
    )
    by_colour, query_dup = lax.optimization_barrier(
        (jnp.asarray(TOKENS_BY_COLOUR, jnp.int32), query_dup)
    )
    by_colour = by_colour[lax.axis_index("head")]
    query_grad = call(
        query_grad_body, [low], new, query_dgate, query_dup, flops=4 * tokens * DH * DH
    )
    blocks, (query_grad,) = with_other(received(blocks, 1), query_grad)
    cots, share, *blocks, back_mid, gate_back, up_back = call(
        ortho_back_body,
        [three, shape(8, WIDE), *quarters, low, low, low],
        *sum_everywhere(blocks),
        kept,
        norm,
        key_rows,
        gate,
        up,
        mid,
        target,
        scalars=by_colour,
        scratch=[three_f32, three_low, three_f32, three_low, whole],
    )
    key_grads = call(
        key_grads_body,
        [low, low],
        cots,
        w_gate,
        w_up,
        w_down,
        step_rates,
        mixed,
        dgate,
        dup,
        back_mid,
        gate_back,
        up_back,
        flops=12 * tokens * DH * DH,
    )
    blocks, (key_grad, value_grad) = with_other(received(blocks, 1), key_grads)
    (quarter,) = call(total_body, quarters[:1], *blocks)
    pieces = lax.all_to_all(
        quarter.reshape(16, 8, WIDE), ALL, 0, 0, axis_index_groups=COLOUR_GROUPS, tiled=True
    )
    grads = call(share_body, [shape(1, 8, DH)] * 3, share, pieces)
    return (query_grad[None], key_grad[None], value_grad[None], *grads)


def solution(mesh):
    split = Mesh(
        mesh.devices.reshape(4, 4, 4, mesh.shape["head"]), ("tok_0", "tok_1", "tok_2", "head")
    )
    rows = P("head", TOK, None)
    weight = P("head", None, None)
    in_specs = (
        rows,
        rows,
        rows,
        P("head", TOK),
        weight,
        weight,
        weight,
        P("head", None),
        rows,
    )
    return jax.shard_map(
        local, mesh=split, in_specs=in_specs, out_specs=(rows,) * 6, check_vma=False
    )
```

```python
import jax
import jax.numpy as jnp
from jax import lax
from jax.experimental import pallas as pl
from jax.experimental.pallas import tpu as pltpu
from jax.sharding import Mesh
from jax.sharding import PartitionSpec as P

TOK = ("tok_0", "tok_1", "tok_2")
ALL = TOK + ("head",)
NS_STEPS = 3
DH = 512
WIDE = 3 * DH
BF = jnp.bfloat16
F32 = jnp.float32
coef_first = 3.4445
coef_second = -4.775
coef_third = 2.0315
inner_step = 0.5
MIB = 1024 * 1024


def flat_at(x, y, z, c):
    return ((x * 4 + y) * 4 + z) * 2 + c


def links(move):
    out = []
    for x in range(4):
        for y in range(4):
            for z in range(4):
                for c in range(2):
                    out.append((flat_at(x, y, z, c), flat_at(*move(x, y, z, c))))
    return out


def pair(i, near):
    return i ^ 1 if near else 3 - i


def partner_links(level, step):
    axis = 3 - step

    def move(x, y, z, c):
        at = [x, y, z]
        at[axis] = pair(at[axis], (level == 1) != (c == 1))
        return (*at, c)

    return links(move)


def antipode_links(step):
    flip = {1: lambda i: 3 - i, 2: lambda i: i ^ 1, 3: lambda i: i ^ 2}[step]
    return links(lambda x, y, z, c: (flip(x), flip(y), flip(z), c))


PARTNERS = {(level, step): partner_links(level, step) for level in (1, 2) for step in (1, 2, 3)}
PARTNERS.update({(3, step): antipode_links(step) for step in (1, 2, 3)})
OTHER_CORE = links(lambda x, y, z, c: (x, y, z, 1 - c))


def colour(x, y, z, low):
    code = 0
    for at in (x, y, z):
        code = 2 * code + (((at + 1) // 2) % 2 if low else at // 2)
    return min(code, 7 - code)


PLACES = [(x, y, z) for x in range(4) for y in range(4) for z in range(4)]


def of_colour(wanted, c):
    return [t for t, at in enumerate(PLACES) if colour(*at, c == 0) == wanted]


COLOUR_GROUPS = [[2 * t + c for t in of_colour(q, c)] for c in range(2) for q in range(4)]
TOKENS_BY_COLOUR = [[t for q in range(4) for t in of_colour(q, c)] for c in range(2)]


def position():
    return [lax.axis_index(a) for a in TOK], lax.axis_index("head")


def own_colour(near):
    at, core = position()
    low, high = 0, 0
    for i in at:
        low = 2 * low + (((i + 1) >> 1) & 1)
        high = 2 * high + (i >> 1)
    code = jnp.where((core == 0) == near, low, high)
    return jnp.where(code >= 4, 7 - code, code)


def own_index():
    (x, y, z), _ = position()
    return (x * 4 + y) * 4 + z


SMEM = pl.BlockSpec(memory_space=pltpu.SMEM)
VMEM = pl.BlockSpec(memory_space=pltpu.VMEM)
HBM = pl.BlockSpec(memory_space=pltpu.HBM)


def call(body, outs, *args, scratch=(), scalars=None, flops=0, specs=None, out_specs=None, limit=3):
    specs = specs or [VMEM] * len(args)
    if scalars is not None:
        specs = [SMEM] + specs
        args = (scalars, *args)
    moved = sum(a.size * a.dtype.itemsize for a in args) + sum(
        o.size * o.dtype.itemsize for o in outs
    )
    return pl.pallas_call(
        body,
        out_shape=list(outs),
        in_specs=specs,
        out_specs=out_specs or [VMEM] * len(outs),
        scratch_shapes=list(scratch),
        compiler_params=pltpu.CompilerParams(vmem_limit_bytes=limit * MIB),
        cost_estimate=pl.CostEstimate(flops=flops, bytes_accessed=moved, transcendentals=0),
    )(*args)


def shape(*dims, dtype=F32):
    return jax.ShapeDtypeStruct(dims, dtype)


def nn(a, b):
    return jnp.dot(a, b, preferred_element_type=F32)


def nt(a, b):
    return lax.dot_general(a, b, (((1,), (1,)), ((), ())), preferred_element_type=F32)


def tn(a, b):
    return lax.dot_general(a, b, (((0,), (0,)), ((), ())), preferred_element_type=F32)


def rows_at(index, rows):
    return pl.ds(pl.multiple_of(index * rows, rows), rows)


def hand_out(own, whole, outs, rows):
    for step in range(4):
        outs[step][...] = whole[rows_at(own ^ step, rows), :]


def columns(index):
    return slice(index * DH, (index + 1) * DH)


def fold_body(a, b, c, d, *outs):
    rows = outs[0].shape[0]
    own = own_colour(False)
    for step in range(4):
        at = rows_at(own ^ step, rows)
        outs[step][...] = (a[at, :] + b[at, :]) + (c[at, :] + d[at, :])


def total_body(*refs):
    *parts, out = refs
    values = [part[...] for part in parts]
    while len(values) > 1:
        values = [values[i] + values[i + 1] for i in range(0, len(values), 2)]
    out[...] = values[0]


def join_body(a, b, c, d, out):
    rows = a.shape[0]
    own = own_colour(False)
    for step, piece in enumerate((a, b, c, d)):
        out[rows_at(own ^ step, rows), :] = piece[...]


def received(blocks, level):
    return [blocks[0]] + [
        lax.ppermute(blocks[step], ALL, PARTNERS[level, step]) for step in (1, 2, 3)
    ]


def with_other(blocks, done):
    return lax.optimization_barrier((tuple(blocks), done))


def sum_everywhere(arrived):
    piece_shape = [shape(32, WIDE)]
    blocks = call(fold_body, piece_shape * 4, *arrived)
    (piece,) = call(total_body, piece_shape, *received(blocks, 2))
    (piece,) = call(total_body, piece_shape, *received([piece] * 4, 3))
    (piece,) = call(join_body, [shape(128, WIDE)], *received([piece] * 4, 2))
    return received([piece] * 4, 1)


def silu_parts(pre_gate):
    sigma_gate = jax.nn.sigmoid(pre_gate)
    act_gate = pre_gate * sigma_gate
    slope_gate = sigma_gate * (1.0 + pre_gate * (1.0 - sigma_gate))
    return (act_gate, slope_gate, sigma_gate)


def as_column(row):
    return jnp.transpose(jnp.broadcast_to(row, (128, row.shape[1])))[:, :1]


def key_body(*refs):
    sources, outs, finals = refs[:6], refs[6:10], refs[10:17]
    copies, stored, whole, in_sems, out_sems = refs[17:23], refs[23:30], *refs[30:]
    moves = [
        pltpu.make_async_copy(source, copy, in_sems.at[i])
        for i, (source, copy) in enumerate(zip(sources, copies))
    ]
    for move in moves:
        move.start()
    keys, w_gate, w_up, rates, values, w_down = copies
    gate, up, mid, mixed, target, dgate, dup = stored
    sent = []
    own = own_colour(True)

    def send(source, goal):
        sent.append(pltpu.make_async_copy(source, goal, out_sems.at[len(sent)]))
        sent[-1].start()

    def keep(index, value):
        stored[index][...] = value
        send(stored[index], finals[index])

    def send_quarters(index):
        for step in range(4):
            at = (rows_at(own ^ step, DH // 4), columns(index))
            send(whole.at[at], outs[step].at[:, columns(index)])

    moves[0].wait()
    moves[1].wait()
    k = keys[...]
    g = nn(k, w_gate[...])
    keep(0, g)
    moves[2].wait()
    u = nn(k, w_up[...])
    keep(1, u)
    act, slope, _ = silu_parts(g)
    mix = (act * u).astype(BF)
    keep(3, mix)
    moves[3].wait()
    moves[4].wait()
    t = (-as_column(rates[...]) * values[...].astype(F32)).astype(BF)
    keep(4, t)
    whole[:, columns(2)] = tn(mix, t)
    send_quarters(2)
    moves[5].wait()
    m = nt(t, w_down[...])
    keep(2, m)
    du = (m * act).astype(BF)
    keep(6, du)
    whole[:, columns(1)] = tn(k, du)
    send_quarters(1)
    dg = (m * u * slope).astype(BF)
    keep(5, dg)
    whole[:, columns(0)] = tn(k, dg)
    send_quarters(0)
    for copy in sent:
        copy.wait()


def query_forward(new, queries, cotangent, gain, stats, output, act_out, slope_out, mixed):
    q = queries[...]
    g = nn(q, new[0])
    u = nn(q, new[1])
    act, slope, _ = silu_parts(g)
    mix = (act * u).astype(BF)
    out = nn(mix, new[2])
    squares = jnp.sum(out * out, axis=1, keepdims=True)
    aligned = jnp.sum(cotangent[...].astype(F32) * gain[...] * out, axis=1, keepdims=True)
    lane = lax.broadcasted_iota(jnp.int32, stats.shape, 1)
    stats[...] = jnp.where(lane == 0, squares, aligned)
    output[...] = out
    act_out[...] = act
    slope_out[...] = u * slope
    mixed[...] = mix


def query_terms_body(
    w_down, queries, cotangent, gain, stats, other, output, act, slope, mixed, *refs
):
    outs, dgate, dup, whole = refs[:4], refs[4], refs[5], refs[6]
    both = stats[...] + other[...]
    inverse_rms = lax.rsqrt(both[:, :1] / (2 * DH) + 1e-05)
    aligned = both[:, 1:2]
    grad_output = (
        gain[...] * cotangent[...].astype(F32) * inverse_rms
        - output[...] * (aligned * inverse_rms * inverse_rms * inverse_rms / (2 * DH))
    ).astype(BF)
    mid = nt(grad_output, w_down[2])
    dg = (mid * slope[...]).astype(BF)
    du = (mid * act[...]).astype(BF)
    dgate[...] = dg
    dup[...] = du
    q = queries[...]
    whole[:, 2 * DH :] = tn(mixed[...], grad_output)
    whole[:, :DH] = tn(q, dg)
    whole[:, DH : 2 * DH] = tn(q, du)
    hand_out(own_colour(True), whole, outs, DH // 4)


def query_grad_body(new, dgate, dup, query_grad):
    query_grad[...] = (nt(dgate[...], new[0]) + nt(dup[...], new[1])).astype(BF)


def key_terms(cots, keys, gate, up, mid, target, back_mid, gate_back, up_back, terms):
    k = keys[...]
    t = target[...]
    back_gate = nn(k, cots[0])
    back_up = nn(k, cots[1])
    back_mixed = nt(t, cots[2])
    g = gate[...]
    u = up[...]
    m = mid[...]
    act, slope, sigma = silu_parts(g)
    curve = sigma * (1.0 - sigma) * (2.0 + g * (1.0 - 2.0 * sigma))
    bm = (back_gate * u * slope + back_up * act).astype(BF)
    gb = (back_gate * m * u * curve + back_up * m * slope + back_mixed * u * slope).astype(BF)
    ub = (back_gate * m * slope + back_mixed * act).astype(BF)
    back_mid[...] = bm
    gate_back[...] = gb
    up_back[...] = ub
    terms[:, :DH] = tn(k, gb)
    terms[:, DH : 2 * DH] = tn(k, ub)
    terms[:, 2 * DH :] = tn(bm, t)


def key_grads_body(
    cots, w_gate, w_up, w_down, rates, mixed, dgate, dup, back_mid, gate_back, up_back, *outs
):
    key_grad, value_grad = outs
    key_grad[...] = (
        nt(dgate[...], cots[0])
        + nt(dup[...], cots[1])
        + nt(gate_back[...], w_gate[...])
        + nt(up_back[...], w_up[...])
    ).astype(BF)
    value_sum = nn(mixed[...], cots[2]) + nn(back_mid[...], w_down[...])
    value_grad[...] = (-as_column(rates[...]) * value_sum).astype(BF)


def share_body(share, pieces, out_a, out_b, out_c):
    value = share[...] + jnp.sum(pieces[...], axis=0)
    for index, out in enumerate((out_a, out_b, out_c)):
        out[0] = value[:, columns(index)]


EACH = range(3)


HALF = DH // 2


def symmetric_product(ref, product, full, added, low):
    value = ref[...]
    for rows, cols in ((slice(0, HALF), slice(0, DH)), (slice(HALF, DH), slice(HALF, DH))):
        other = value[cols] if product is nt else value[:, cols]
        block = product(value[rows], other)
        if added is not None:
            block = coef_second * added[rows, cols] + coef_third * block
        if full is not None:
            full[rows, cols] = block
        low[rows, cols] = block.astype(BF)
    low[HALF:, :HALF] = jnp.transpose(low[:HALF, HALF:])


def ortho_body(a, b, c, d, w_gate, w_up, w_down, queries, cotangent, gain, *refs):
    new, kept, norm, query_refs, (current, gram) = refs[0], refs[1], refs[2], refs[3:8], refs[8:]
    own = own_colour(True)
    for step, block in enumerate((a, b, c, d)):
        for i in EACH:
            current[i, rows_at(own ^ step, DH // 4), :] = block[:, columns(i)]
    for i in EACH:
        matrix = current[i]
        root = jnp.sqrt(jnp.sum(matrix * matrix, keepdims=True) + 1e-06)
        norm[i] = jnp.broadcast_to(root, norm.shape[1:])
        unit = matrix * (1.0 / root)
        current[i] = unit
        kept[i, 0] = unit.astype(BF)
    for step in range(NS_STEPS):
        for i in EACH:
            symmetric_product(kept.at[i, 3 * step], nt, gram.at[i], None, kept.at[i, 3 * step + 1])
        for i in EACH:
            symmetric_product(kept.at[i, 3 * step + 1], nn, None, gram.at[i], kept.at[i, 3 * step + 2])
        for i, weight in enumerate((w_gate, w_up, w_down)):
            later = coef_first * current[i] + nn(kept[i, 3 * step + 2], kept[i, 3 * step])
            if step < NS_STEPS - 1:
                current[i] = later
                kept[i, 3 * step + 3] = later.astype(BF)
            else:
                new[i] = (weight[...].astype(F32) - inner_step * later).astype(BF)
    query_forward(new, queries, cotangent, gain, *query_refs)


def ortho_back_body(by_colour, a, b, c, d, kept, norm, keys, gate, up, mid, target, *refs):
    cots, share, outs, key_refs = refs[0], refs[1], refs[2:6], refs[6:9]
    grad, grad_low, half, sym, terms = refs[9:]
    near = own_colour(True)
    for step, block in enumerate((a, b, c, d)):
        for i in EACH:
            grad[i, rows_at(near ^ step, DH // 4), :] = block[:, columns(i)]
    for i in EACH:
        share[:, columns(i)] = grad[i, rows_at(own_index(), 8), :]
        start = grad[i] * (-inner_step)
        grad[i] = start
        grad_low[i] = start.astype(BF)
    for step in reversed(range(NS_STEPS)):
        for i in EACH:
            half[i] = nt(grad_low[i], kept[i, 3 * step])
        for i in EACH:
            both = half[i] + jnp.transpose(half[i])
            sym[i] = both.astype(BF)
        for i in EACH:
            half[i] = coef_third * nn(sym[i], kept[i, 3 * step + 1])
        for i in EACH:
            full = coef_second * sym[i].astype(F32) + (half[i] + jnp.transpose(half[i]))
            sym[i] = full.astype(BF)
        for i in EACH:
            later = (
                coef_first * grad[i]
                + nn(kept[i, 3 * step + 2], grad_low[i])
                + nn(sym[i], kept[i, 3 * step])
            )
            grad[i] = later
            if step > 0:
                grad_low[i] = later.astype(BF)
    for i in EACH:
        unit = kept[i, 0].astype(F32)
        along = jnp.sum(grad[i] * unit, keepdims=True)
        cots[i] = ((grad[i] - unit * along) * (1.0 / norm[i, :1, :1])).astype(BF)
    key_terms(cots, keys, gate, up, mid, target, *key_refs, terms)
    for step in range(4):
        first = 16 * (near ^ step)
        for j in range(16):
            outs[step][8 * j : 8 * j + 8, :] = terms[rows_at(by_colour[first + j], 8), :]


def local(queries, key_rows, value_rows, step_rates, w_gate, w_up, w_down, out_gain, cotangent):
    tokens = queries.shape[1]
    queries, key_rows, value_rows, cotangent = (
        a[0] for a in (queries, key_rows, value_rows, cotangent)
    )
    w_gate, w_up, w_down = w_gate[0], w_up[0], w_down[0]
    whole = pltpu.VMEM((DH, WIDE), F32)
    quarters = [shape(DH // 4, WIDE)] * 4
    wide = shape(tokens, DH)
    low = shape(tokens, DH, dtype=BF)
    three = shape(3, DH, DH, dtype=BF)
    three_f32 = pltpu.VMEM((3, DH, DH), F32)
    three_low = pltpu.VMEM((3, DH, DH), BF)
    key_inputs = (key_rows, w_gate, w_up, step_rates, value_rows, w_down)
    stored_shapes = [wide, wide, wide, low, low, low, low]
    *blocks, gate, up, mid, mixed, target, dgate, dup = call(
        key_body,
        [*quarters, *stored_shapes],
        *key_inputs,
        scratch=[
            *(pltpu.VMEM(a.shape, a.dtype) for a in (*key_inputs, *stored_shapes)),
            whole,
            pltpu.SemaphoreType.DMA((6,)),
            pltpu.SemaphoreType.DMA((19,)),
        ],
        specs=[HBM] * 6,
        out_specs=[HBM] * 11,
        limit=56,
    )
    arrived, (mine,) = with_other(received(blocks, 1), call(total_body, quarters[:1], blocks[0]))
    arrived = (mine, *arrived[1:])
    new, kept, norm, stats, *query_stored = call(
        ortho_body,
        [
            three,
            shape(3, 9, DH, DH, dtype=BF),
            shape(3, 8, 128),
            shape(tokens, 128),
            wide,
            wide,
            wide,
            low,
        ],
        *sum_everywhere(arrived),
        w_gate,
        w_up,
        w_down,
        queries,
        cotangent,
        out_gain,
        scratch=[three_f32, three_f32],
        limit=14,
    )
    other = lax.ppermute(stats, ALL, OTHER_CORE)
    *blocks, query_dgate, query_dup = call(
        query_terms_body,
        [*quarters, low, low],
        new,
        queries,
        cotangent,
        out_gain,
        stats,
        other,
        *query_stored,
        scratch=[whole],
        limit=8,
    )
    by_colour, query_dup = lax.optimization_barrier(
        (jnp.asarray(TOKENS_BY_COLOUR, jnp.int32), query_dup)
    )
    by_colour = by_colour[lax.axis_index("head")]
    query_grad = call(
        query_grad_body, [low], new, query_dgate, query_dup, flops=4 * tokens * DH * DH, limit=4
    )
    blocks, (query_grad,) = with_other(received(blocks, 1), query_grad)
    cots, share, *blocks, back_mid, gate_back, up_back = call(
        ortho_back_body,
        [three, shape(8, WIDE), *quarters, low, low, low],
        *sum_everywhere(blocks),
        kept,
        norm,
        key_rows,
        gate,
        up,
        mid,
        target,
        scalars=by_colour,
        scratch=[three_f32, three_low, three_f32, three_low, whole],
        limit=20,
    )
    key_grads = call(
        key_grads_body,
        [low, low],
        cots,
        w_gate,
        w_up,
        w_down,
        step_rates,
        mixed,
        dgate,
        dup,
        back_mid,
        gate_back,
        up_back,
        flops=12 * tokens * DH * DH,
        limit=6,
    )
    blocks, (key_grad, value_grad) = with_other(received(blocks, 1), key_grads)
    (quarter,) = call(total_body, quarters[:1], *blocks)
    pieces = lax.all_to_all(
        quarter.reshape(16, 8, WIDE), ALL, 0, 0, axis_index_groups=COLOUR_GROUPS, tiled=True
    )
    grads = call(share_body, [shape(1, 8, DH)] * 3, share, pieces)
    return (query_grad[None], key_grad[None], value_grad[None], *grads)


def solution(mesh):
    split = Mesh(
        mesh.devices.reshape(4, 4, 4, mesh.shape["head"]), ("tok_0", "tok_1", "tok_2", "head")
    )
    rows = P("head", TOK, None)
    weight = P("head", None, None)
    in_specs = (
        rows,
        rows,
        rows,
        P("head", TOK),
        weight,
        weight,
        weight,
        P("head", None),
        rows,
    )
    return jax.shard_map(
        local, mesh=split, in_specs=in_specs, out_specs=(rows,) * 6, check_vma=False
    )
```

```python
import jax
import jax.numpy as jnp
from jax import lax
from jax.experimental import pallas as pl
from jax.experimental.pallas import tpu as pltpu
from jax.sharding import Mesh
from jax.sharding import PartitionSpec as P

TOK = ("tok_0", "tok_1", "tok_2")
ALL = TOK + ("head",)
NS_STEPS = 3
DH = 512
WIDE = 3 * DH
BF = jnp.bfloat16
F32 = jnp.float32
coef_first = 3.4445
coef_second = -4.775
coef_third = 2.0315
inner_step = 0.5
MIB = 1024 * 1024


def flat_at(x, y, z, c):
    return ((x * 4 + y) * 4 + z) * 2 + c


def links(move):
    out = []
    for x in range(4):
        for y in range(4):
            for z in range(4):
                for c in range(2):
                    out.append((flat_at(x, y, z, c), flat_at(*move(x, y, z, c))))
    return out


def pair(i, near):
    return i ^ 1 if near else 3 - i


def partner_links(level, step):
    axis = 3 - step

    def move(x, y, z, c):
        at = [x, y, z]
        at[axis] = pair(at[axis], (level == 1) != (c == 1))
        return (*at, c)

    return links(move)


def antipode_links(step):
    flip = {1: lambda i: 3 - i, 2: lambda i: i ^ 1, 3: lambda i: i ^ 2}[step]
    return links(lambda x, y, z, c: (flip(x), flip(y), flip(z), c))


PARTNERS = {(level, step): partner_links(level, step) for level in (1, 2) for step in (1, 2, 3)}
PARTNERS.update({(3, step): antipode_links(step) for step in (1, 2, 3)})
OTHER_CORE = links(lambda x, y, z, c: (x, y, z, 1 - c))


def colour(x, y, z, low):
    code = 0
    for at in (x, y, z):
        code = 2 * code + (((at + 1) // 2) % 2 if low else at // 2)
    return min(code, 7 - code)


PLACES = [(x, y, z) for x in range(4) for y in range(4) for z in range(4)]


def of_colour(wanted, c):
    return [t for t, at in enumerate(PLACES) if colour(*at, c == 0) == wanted]


COLOUR_GROUPS = [[2 * t + c for t in of_colour(q, c)] for c in range(2) for q in range(4)]
TOKENS_BY_COLOUR = [[t for q in range(4) for t in of_colour(q, c)] for c in range(2)]


def position():
    return [lax.axis_index(a) for a in TOK], lax.axis_index("head")


def own_colour(near):
    at, core = position()
    low, high = 0, 0
    for i in at:
        low = 2 * low + (((i + 1) >> 1) & 1)
        high = 2 * high + (i >> 1)
    code = jnp.where((core == 0) == near, low, high)
    return jnp.where(code >= 4, 7 - code, code)


def own_index():
    (x, y, z), _ = position()
    return (x * 4 + y) * 4 + z


SMEM = pl.BlockSpec(memory_space=pltpu.SMEM)
VMEM = pl.BlockSpec(memory_space=pltpu.VMEM)
HBM = pl.BlockSpec(memory_space=pltpu.HBM)


def call(body, outs, *args, scratch=(), scalars=None, flops=0, specs=None, out_specs=None, limit=3):
    specs = specs or [VMEM] * len(args)
    if scalars is not None:
        specs = [SMEM] + specs
        args = (scalars, *args)
    moved = sum(a.size * a.dtype.itemsize for a in args) + sum(
        o.size * o.dtype.itemsize for o in outs
    )
    return pl.pallas_call(
        body,
        out_shape=list(outs),
        in_specs=specs,
        out_specs=out_specs or [VMEM] * len(outs),
        scratch_shapes=list(scratch),
        compiler_params=pltpu.CompilerParams(vmem_limit_bytes=limit * MIB),
        cost_estimate=pl.CostEstimate(flops=flops, bytes_accessed=moved, transcendentals=0),
    )(*args)


def shape(*dims, dtype=F32):
    return jax.ShapeDtypeStruct(dims, dtype)


def nn(a, b):
    return jnp.dot(a, b, preferred_element_type=F32)


def nt(a, b):
    return lax.dot_general(a, b, (((1,), (1,)), ((), ())), preferred_element_type=F32)


def tn(a, b):
    return lax.dot_general(a, b, (((0,), (0,)), ((), ())), preferred_element_type=F32)


def rows_at(index, rows):
    return pl.ds(pl.multiple_of(index * rows, rows), rows)


def hand_out(own, whole, outs, rows):
    for step in range(4):
        outs[step][...] = whole[rows_at(own ^ step, rows), :]


def columns(index):
    return slice(index * DH, (index + 1) * DH)


def fold_body(a, b, c, d, *outs):
    rows = outs[0].shape[0]
    own = own_colour(False)
    for step in range(4):
        at = rows_at(own ^ step, rows)
        outs[step][...] = (a[at, :] + b[at, :]) + (c[at, :] + d[at, :])


def total_body(*refs):
    *parts, out = refs
    values = [part[...] for part in parts]
    while len(values) > 1:
        values = [values[i] + values[i + 1] for i in range(0, len(values), 2)]
    out[...] = values[0]


def join_body(a, b, c, d, out):
    rows = a.shape[0]
    own = own_colour(False)
    for step, piece in enumerate((a, b, c, d)):
        out[rows_at(own ^ step, rows), :] = piece[...]


def received(blocks, level):
    return [blocks[0]] + [
        lax.ppermute(blocks[step], ALL, PARTNERS[level, step]) for step in (1, 2, 3)
    ]


def with_other(blocks, done):
    return lax.optimization_barrier((tuple(blocks), done))


def sum_everywhere(arrived):
    piece_shape = [shape(32, WIDE)]
    blocks = call(fold_body, piece_shape * 4, *arrived)
    (piece,) = call(total_body, piece_shape, *received(blocks, 2))
    (piece,) = call(total_body, piece_shape, *received([piece] * 4, 3))
    (piece,) = call(join_body, [shape(128, WIDE)], *received([piece] * 4, 2))
    return received([piece] * 4, 1)


def silu_parts(pre_gate):
    sigma_gate = jax.nn.sigmoid(pre_gate)
    act_gate = pre_gate * sigma_gate
    slope_gate = sigma_gate * (1.0 + pre_gate * (1.0 - sigma_gate))
    return (act_gate, slope_gate, sigma_gate)


def as_column(row):
    return jnp.transpose(jnp.broadcast_to(row, (128, row.shape[1])))[:, :1]


def key_body(*refs):
    sources, outs, finals = refs[:6], refs[6:10], refs[10:17]
    copies, stored, whole, in_sems, out_sems = refs[17:23], refs[23:30], *refs[30:]
    moves = [
        pltpu.make_async_copy(source, copy, in_sems.at[i])
        for i, (source, copy) in enumerate(zip(sources, copies))
    ]
    for move in moves:
        move.start()
    keys, w_gate, w_up, rates, values, w_down = copies
    gate, up, mid, mixed, target, dgate, dup = stored
    sent = []
    own = own_colour(True)

    def send(source, goal):
        sent.append(pltpu.make_async_copy(source, goal, out_sems.at[len(sent)]))
        sent[-1].start()

    def keep(index, value):
        stored[index][...] = value
        send(stored[index], finals[index])

    def send_quarters(index):
        for step in range(4):
            at = (rows_at(own ^ step, DH // 4), columns(index))
            send(whole.at[at], outs[step].at[:, columns(index)])

    moves[0].wait()
    moves[1].wait()
    k = keys[...]
    g = nn(k, w_gate[...])
    keep(0, g)
    moves[2].wait()
    u = nn(k, w_up[...])
    keep(1, u)
    act, slope, _ = silu_parts(g)
    mix = (act * u).astype(BF)
    keep(3, mix)
    moves[3].wait()
    moves[4].wait()
    t = (-as_column(rates[...]) * values[...].astype(F32)).astype(BF)
    keep(4, t)
    whole[:, columns(2)] = tn(mix, t)
    send_quarters(2)
    moves[5].wait()
    m = nt(t, w_down[...])
    keep(2, m)
    du = (m * act).astype(BF)
    keep(6, du)
    whole[:, columns(1)] = tn(k, du)
    send_quarters(1)
    dg = (m * u * slope).astype(BF)
    keep(5, dg)
    whole[:, columns(0)] = tn(k, dg)
    send_quarters(0)
    for copy in sent:
        copy.wait()


def query_forward(new, queries, cotangent, gain, stats, output, act_out, slope_out, mixed):
    q = queries[...]
    g = nn(q, new[0])
    u = nn(q, new[1])
    act, slope, _ = silu_parts(g)
    mix = (act * u).astype(BF)
    out = nn(mix, new[2])
    squares = jnp.sum(out * out, axis=1, keepdims=True)
    aligned = jnp.sum(cotangent[...].astype(F32) * gain[...] * out, axis=1, keepdims=True)
    lane = lax.broadcasted_iota(jnp.int32, stats.shape, 1)
    stats[...] = jnp.where(lane == 0, squares, aligned)
    output[...] = out
    act_out[...] = act
    slope_out[...] = u * slope
    mixed[...] = mix


def query_terms_body(
    w_down, queries, cotangent, gain, stats, other, output, act, slope, mixed, *refs
):
    outs, dgate, dup, whole = refs[:4], refs[4], refs[5], refs[6]
    both = stats[...] + other[...]
    inverse_rms = lax.rsqrt(both[:, :1] / (2 * DH) + 1e-05)
    aligned = both[:, 1:2]
    grad_output = (
        gain[...] * cotangent[...].astype(F32) * inverse_rms
        - output[...] * (aligned * inverse_rms * inverse_rms * inverse_rms / (2 * DH))
    ).astype(BF)
    mid = nt(grad_output, w_down[2])
    dg = (mid * slope[...]).astype(BF)
    du = (mid * act[...]).astype(BF)
    dgate[...] = dg
    dup[...] = du
    q = queries[...]
    whole[:, 2 * DH :] = tn(mixed[...], grad_output)
    whole[:, :DH] = tn(q, dg)
    whole[:, DH : 2 * DH] = tn(q, du)
    hand_out(own_colour(True), whole, outs, DH // 4)


def query_grad_body(new, dgate, dup, query_grad):
    query_grad[...] = (nt(dgate[...], new[0]) + nt(dup[...], new[1])).astype(BF)


def key_terms(cots, keys, gate, up, mid, target, back_mid, gate_back, up_back, terms):
    k = keys[...]
    t = target[...]
    back_gate = nn(k, cots[0])
    back_up = nn(k, cots[1])
    back_mixed = nt(t, cots[2])
    g = gate[...]
    u = up[...]
    m = mid[...]
    act, slope, sigma = silu_parts(g)
    curve = sigma * (1.0 - sigma) * (2.0 + g * (1.0 - 2.0 * sigma))
    bm = (back_gate * u * slope + back_up * act).astype(BF)
    gb = (back_gate * m * u * curve + back_up * m * slope + back_mixed * u * slope).astype(BF)
    ub = (back_gate * m * slope + back_mixed * act).astype(BF)
    back_mid[...] = bm
    gate_back[...] = gb
    up_back[...] = ub
    terms[:, :DH] = tn(k, gb)
    terms[:, DH : 2 * DH] = tn(k, ub)
    terms[:, 2 * DH :] = tn(bm, t)


def key_grads_body(
    cots, w_gate, w_up, w_down, rates, mixed, dgate, dup, back_mid, gate_back, up_back, *outs
):
    key_grad, value_grad = outs
    key_grad[...] = (
        nt(dgate[...], cots[0])
        + nt(dup[...], cots[1])
        + nt(gate_back[...], w_gate[...])
        + nt(up_back[...], w_up[...])
    ).astype(BF)
    value_sum = nn(mixed[...], cots[2]) + nn(back_mid[...], w_down[...])
    value_grad[...] = (-as_column(rates[...]) * value_sum).astype(BF)


def share_body(share, pieces, out_a, out_b, out_c):
    value = share[...] + jnp.sum(pieces[...], axis=0)
    for index, out in enumerate((out_a, out_b, out_c)):
        out[0] = value[:, columns(index)]


EACH = range(3)


HALF = DH // 2


def symmetric_product(ref, product, full, added, low):
    value = ref[...]
    for rows, cols in ((slice(0, HALF), slice(0, DH)), (slice(HALF, DH), slice(HALF, DH))):
        other = value[cols] if product is nt else value[:, cols]
        block = product(value[rows], other)
        if added is not None:
            block = coef_second * added[rows, cols] + coef_third * block
        if full is not None:
            full[rows, cols] = block
        low[rows, cols] = block.astype(BF)
    low[HALF:, :HALF] = jnp.transpose(low[:HALF, HALF:])


def ortho_body(a, b, c, d, w_gate, w_up, w_down, queries, cotangent, gain, *refs):
    new, kept, norm, query_refs, (current, gram) = refs[0], refs[1], refs[2], refs[3:8], refs[8:]
    own = own_colour(True)
    for step, block in enumerate((a, b, c, d)):
        for i in EACH:
            current[i, rows_at(own ^ step, DH // 4), :] = block[:, columns(i)]
    for i in EACH:
        matrix = current[i]
        root = jnp.sqrt(jnp.sum(matrix * matrix, keepdims=True) + 1e-06)
        norm[i] = jnp.broadcast_to(root, norm.shape[1:])
        unit = matrix * (1.0 / root)
        current[i] = unit
        kept[i, 0] = unit.astype(BF)
    for step in range(NS_STEPS):
        for i in EACH:
            symmetric_product(kept.at[i, 3 * step], nt, gram.at[i], None, kept.at[i, 3 * step + 1])
        for i in EACH:
            symmetric_product(kept.at[i, 3 * step + 1], nn, None, gram.at[i], kept.at[i, 3 * step + 2])
        for i, weight in enumerate((w_gate, w_up, w_down)):
            later = coef_first * current[i] + nn(kept[i, 3 * step + 2], kept[i, 3 * step])
            if step < NS_STEPS - 1:
                current[i] = later
                kept[i, 3 * step + 3] = later.astype(BF)
            else:
                new[i] = (weight[...].astype(F32) - inner_step * later).astype(BF)
    query_forward(new, queries, cotangent, gain, *query_refs)


def ortho_back_body(by_colour, a, b, c, d, kept, norm, keys, gate, up, mid, target, *refs):
    cots, share, outs, key_refs = refs[0], refs[1], refs[2:6], refs[6:9]
    grad, grad_low, half, sym, terms = refs[9:]
    near = own_colour(True)
    for step, block in enumerate((a, b, c, d)):
        for i in EACH:
            grad[i, rows_at(near ^ step, DH // 4), :] = block[:, columns(i)]
    for i in EACH:
        share[:, columns(i)] = grad[i, rows_at(own_index(), 8), :]
        start = grad[i] * (-inner_step)
        grad[i] = start
        grad_low[i] = start.astype(BF)
    for step in reversed(range(NS_STEPS)):
        for i in EACH:
            half[i] = nt(grad_low[i], kept[i, 3 * step])
        for i in EACH:
            both = half[i] + jnp.transpose(half[i])
            sym[i] = both.astype(BF)
        for i in EACH:
            half[i] = coef_third * nn(sym[i], kept[i, 3 * step + 1])
        for i in EACH:
            full = coef_second * sym[i].astype(F32) + (half[i] + jnp.transpose(half[i]))
            sym[i] = full.astype(BF)
        for i in EACH:
            later = (
                coef_first * grad[i]
                + nn(kept[i, 3 * step + 2], grad_low[i])
                + nn(sym[i], kept[i, 3 * step])
            )
            grad[i] = later
            if step > 0:
                grad_low[i] = later.astype(BF)
    for i in EACH:
        unit = kept[i, 0].astype(F32)
        along = jnp.sum(grad[i] * unit, keepdims=True)
        cots[i] = ((grad[i] - unit * along) * (1.0 / norm[i, :1, :1])).astype(BF)
    key_terms(cots, keys, gate, up, mid, target, *key_refs, terms)
    for step in range(4):
        first = 16 * (near ^ step)
        core = lax.axis_index("head")
        for j in range(16):
            outs[step][8 * j : 8 * j + 8, :] = terms[rows_at(by_colour[core, first + j], 8), :]


def local(queries, key_rows, value_rows, step_rates, w_gate, w_up, w_down, out_gain, cotangent):
    tokens = queries.shape[1]
    queries, key_rows, value_rows, cotangent = (
        a[0] for a in (queries, key_rows, value_rows, cotangent)
    )
    w_gate, w_up, w_down = w_gate[0], w_up[0], w_down[0]
    whole = pltpu.VMEM((DH, WIDE), F32)
    quarters = [shape(DH // 4, WIDE)] * 4
    wide = shape(tokens, DH)
    low = shape(tokens, DH, dtype=BF)
    three = shape(3, DH, DH, dtype=BF)
    three_f32 = pltpu.VMEM((3, DH, DH), F32)
    three_low = pltpu.VMEM((3, DH, DH), BF)
    key_inputs = (key_rows, w_gate, w_up, step_rates, value_rows, w_down)
    stored_shapes = [wide, wide, wide, low, low, low, low]
    *blocks, gate, up, mid, mixed, target, dgate, dup = call(
        key_body,
        [*quarters, *stored_shapes],
        *key_inputs,
        scratch=[
            *(pltpu.VMEM(a.shape, a.dtype) for a in (*key_inputs, *stored_shapes)),
            whole,
            pltpu.SemaphoreType.DMA((6,)),
            pltpu.SemaphoreType.DMA((19,)),
        ],
        specs=[HBM] * 6,
        out_specs=[HBM] * 11,
        limit=56,
    )
    arrived, (mine,) = with_other(received(blocks, 1), call(total_body, quarters[:1], blocks[0]))
    arrived = (mine, *arrived[1:])
    new, kept, norm, stats, *query_stored = call(
        ortho_body,
        [
            three,
            shape(3, 9, DH, DH, dtype=BF),
            shape(3, 8, 128),
            shape(tokens, 128),
            wide,
            wide,
            wide,
            low,
        ],
        *sum_everywhere(arrived),
        w_gate,
        w_up,
        w_down,
        queries,
        cotangent,
        out_gain,
        scratch=[three_f32, three_f32],
        limit=14,
    )
    other = lax.ppermute(stats, ALL, OTHER_CORE)
    *blocks, query_dgate, query_dup = call(
        query_terms_body,
        [*quarters, low, low],
        new,
        queries,
        cotangent,
        out_gain,
        stats,
        other,
        *query_stored,
        scratch=[whole],
        limit=8,
    )
    query_grad = call(
        query_grad_body, [low], new, query_dgate, query_dup, flops=4 * tokens * DH * DH, limit=4
    )
    blocks, (query_grad,) = with_other(received(blocks, 1), query_grad)
    cots, share, *blocks, back_mid, gate_back, up_back = call(
        ortho_back_body,
        [three, shape(8, WIDE), *quarters, low, low, low],
        *sum_everywhere(blocks),
        kept,
        norm,
        key_rows,
        gate,
        up,
        mid,
        target,
        scalars=jnp.asarray(TOKENS_BY_COLOUR, jnp.int32),
        scratch=[three_f32, three_low, three_f32, three_low, whole],
        limit=20,
    )
    key_grads = call(
        key_grads_body,
        [low, low],
        cots,
        w_gate,
        w_up,
        w_down,
        step_rates,
        mixed,
        dgate,
        dup,
        back_mid,
        gate_back,
        up_back,
        flops=12 * tokens * DH * DH,
        limit=6,
    )
    blocks, (key_grad, value_grad) = with_other(received(blocks, 1), key_grads)
    (quarter,) = call(total_body, quarters[:1], *blocks)
    pieces = lax.all_to_all(
        quarter.reshape(16, 8, WIDE), ALL, 0, 0, axis_index_groups=COLOUR_GROUPS, tiled=True
    )
    grads = call(share_body, [shape(1, 8, DH)] * 3, share, pieces)
    return (query_grad[None], key_grad[None], value_grad[None], *grads)


def solution(mesh):
    split = Mesh(
        mesh.devices.reshape(4, 4, 4, mesh.shape["head"]), ("tok_0", "tok_1", "tok_2", "head")
    )
    rows = P("head", TOK, None)
    weight = P("head", None, None)
    in_specs = (
        rows,
        rows,
        rows,
        P("head", TOK),
        weight,
        weight,
        weight,
        P("head", None),
        rows,
    )
    return jax.shard_map(
        local, mesh=split, in_specs=in_specs, out_specs=(rows,) * 6, check_vma=False
    )
```
